512 devices in a mesh: vocab: 32 (over x, z), dp: 16 (over y, core).
Axes of the slice: x: 4, y: 8, z: 8, core: 2. Of those that a mesh axis runs over, the one named last changes fastest.
Arguments:
- out_grads: float32 [65536, 4096], P(('vocab', 'dp')), may hold values from -6 to 6
- token_ids: int32 [65536], P(('vocab', 'dp')), may hold values from 0 to 128255, as said below
Outputs:
- table_grad: bfloat16 [128256, 4096], P('vocab', 'dp')
The draws below stay inside these ranges and needn't reach their ends.
Inputs may be any that keep to these rules, and one draw needn't show every extreme that they name: `token_ids`: call ids k * 4008 to (k + 1) * 4008 - 1 block k. The 128 tokens of one device hold at most 12 ids of any one block; one block, the same for all devices, holds exactly 12 ids of every device.
All inputs are finite; a program needn't handle non-finite values.
Results may differ from the reference program's by a relative error of at most 0.001.
Values sent between devices are 32-bit elements; how exact they have to be, the bound alone decides.
No kernel may reach another device: no remote copies, remote signals or barrier semaphores. Data moves between devices by JAX's collectives and lax.ppermute only.
A program may use at most 64 MiB of HBM per device.

```python
import jax
import jax.numpy as jnp
from jax import lax

D = 4096
VOCAB = 128256
TOK_DEV = 128
TOKENS = 65536
N_VOCAB = 32
N_DP = 16


def draw_token_ids(key, part):
    rows_own = VOCAB // N_VOCAB
    capacity = 3 * TOK_DEV // N_VOCAB
    key_hot, key_rest = jax.random.split(jax.random.fold_in(key, 71))
    hot_block = jax.random.randint(key_hot, (), 0, N_VOCAB).astype(jnp.int32)

    def one_device(sub_key):
        key_pick, key_order, key_first, key_second = jax.random.split(sub_key, 4)
        others = (hot_block + 1 + jnp.arange((N_VOCAB - 1) * capacity, dtype=jnp.int32) // capacity) % N_VOCAB
        picked = jax.random.permutation(key_pick, others)[:TOK_DEV - capacity]
        owners = jnp.concatenate([jnp.full((capacity,), hot_block, jnp.int32), picked.astype(jnp.int32)])
        owners = jax.random.permutation(key_order, owners)
        first = jax.random.randint(key_first, (TOK_DEV,), 0, rows_own).astype(jnp.int32)
        second = jax.random.randint(key_second, (TOK_DEV,), 0, rows_own).astype(jnp.int32)
        inside = first * second // rows_own
        return (owners * rows_own + inside).astype(jnp.int32)
    device_keys = jax.random.split(key_rest, N_VOCAB * N_DP)
    return jax.vmap(one_device)(device_keys).reshape(-1).astype(jnp.int32)


def level_of(rng, shape, cuts, low, top_value):
    loudness = 1.0
    for axis_at, shards_of in cuts:
        heights = jax.random.uniform(jax.random.fold_in(jax.random.fold_in(rng, 6), axis_at), (shards_of,), jnp.float32, low / len(cuts), top_value / len(cuts))
        loudness = loudness * jnp.repeat(jnp.exp(heights), shape[axis_at] // shards_of).reshape((-1,) + (1,) * (len(shape) - 1 - axis_at))
    return loudness


def centred(rng, shape, spread, most, shards=(), kind=jnp.bfloat16):
    factor_of = level_of(rng, shape, shards, -0.22, 0.18) if shards else 1.0
    result = jax.random.normal(rng, shape, jnp.float32) * spread * factor_of
    return jnp.minimum(jnp.maximum(result, -most), most).astype(kind)


def setup_inputs(seed: int = 0) -> dict:
    streams_of = jax.random.split(jax.random.key(seed), 3)
    out_grads = centred(streams_of[0], (TOKENS, D), 1.0, 6.0, ((0, 512),), jnp.float32)
    token_ids = draw_token_ids(jax.random.fold_in(streams_of[2], 71), 0)
    return dict(out_grads=out_grads, token_ids=token_ids)


def reference(out_grads, token_ids):
    width_block = 256 if D % 256 == 0 else D
    blocks = D // width_block
    pieces = out_grads.reshape(TOKENS, blocks, width_block).transpose(1, 0, 2)

    def one_block(piece):
        summed = jax.ops.segment_sum(piece, token_ids, num_segments=VOCAB)
        return summed.astype(jnp.bfloat16)

    table = lax.map(one_block, pieces)
    return table.transpose(1, 0, 2).reshape(VOCAB, D)
```

```python
import functools

import jax
import jax.numpy as jnp
from jax import lax
from jax.experimental import pallas as pl
from jax.experimental.pallas import tpu as pltpu
from jax.sharding import PartitionSpec as P

VOCAB = 128256
LANES = 128
ROW = 256
HEAD = 8
SLOTS = 88
COUNT, SPILL = 254, 255
PARAMS = pltpu.CompilerParams(vmem_limit_bytes=52 * 2**20)


def iota(shape, dim):
    return lax.broadcasted_iota(jnp.int32, shape, dim)


def head_kernel(cap, ids_ref, owner_ref, ids_row_ref, x_ref, head_ref, body_ref, count_ref, pick_ref):
    tok, width = x_ref.shape
    parts = width // ROW
    owners, early = count_ref.shape[0], pick_ref.shape[0]

    def zero(i, carry):
        count_ref[i] = 0
        return carry

    lax.fori_loop(0, owners, zero, 0)
    for j in range(early):
        pick_ref[j] = 0

    def tally(t, full):
        o = owner_ref[t]
        c = count_ref[o] + 1
        count_ref[o] = c
        return jnp.where(c == cap, o, full)

    full = lax.fori_loop(0, tok, tally, -1)

    def pick(t, j):
        @pl.when((owner_ref[t] == full) & (j < early))
        def _():
            pick_ref[j] = t

        return j + (owner_ref[t] == full).astype(jnp.int32)

    lax.fori_loop(0, tok, pick, 0)
    lane = iota((1, LANES), 1)
    note = jnp.where(lane == early, full.astype(jnp.float32), 0.0)
    for j in range(early):
        t = pick_ref[j]
        note = jnp.where(lane == j, ids_ref[t].astype(jnp.float32), note)
        row = x_ref[pl.ds(t, 1), :]
        for d in range(parts):
            head_ref[d, j : j + 1, :] = row[:, d * ROW : (d + 1) * ROW]
    for d in range(parts):
        head_ref[d, early:HEAD, 0:LANES] = ids_row_ref[...]
        head_ref[d, early:HEAD, LANES:ROW] = note
        body_ref[d] = x_ref[:, d * ROW : (d + 1) * ROW]


def head(ids, owner, x, cap, owners):
    tok, width = x.shape
    parts = width // ROW
    smem, vmem = pl.BlockSpec(memory_space=pltpu.SMEM), pl.BlockSpec(memory_space=pltpu.VMEM)
    return pl.pallas_call(
        functools.partial(head_kernel, cap),
        out_shape=(
            jax.ShapeDtypeStruct((parts, HEAD, ROW), jnp.float32),
            jax.ShapeDtypeStruct((parts, tok, ROW), jnp.float32),
        ),
        in_specs=[smem, smem, vmem, vmem],
        out_specs=(vmem, vmem),
        scratch_shapes=[pltpu.SMEM((owners,), jnp.int32), pltpu.SMEM((HEAD - 1,), jnp.int32)],
        compiler_params=PARAMS,
        name="head",
    )(ids, owner, ids.astype(jnp.float32)[None, :], x)


def plan(ids, full, early, rows_own, owners):
    sources, tok = ids.shape
    own = ids // rows_own
    fits = own == full[:, None]
    nth = jnp.sum((fits[:, None, :] & (iota((1, tok, tok), 2) < iota((1, tok, tok), 1))).astype(jnp.int32), axis=2)
    mine = ~fits | (nth >= early)
    hit = ((own[:, :, None] == iota((1, 1, owners), 2)) & mine[:, :, None]).astype(jnp.float32)
    tri = (iota((tok, tok), 1) < iota((tok, tok), 0)).astype(jnp.float32)
    inside = jnp.einsum("ts,dsk->dtk", tri, hit)
    count = jnp.sum(hit, axis=1)
    before = jnp.sum(
        jnp.where((iota((sources, sources), 1) < iota((sources, sources), 0))[:, :, None], count[None], 0.0), axis=1
    )
    slot = jnp.sum(hit * (inside + before[:, None, :]), axis=2).astype(jnp.int32)
    total = jnp.sum(count, axis=0)
    return own, mine, hit, slot, total


def id_rows(hit, slot, local, total, lo, hi, rows_own, spill):
    n = hi - lo
    owners = hit.shape[2]
    at = (slot[:, :, None] - lo == iota((1, 1, ROW), 2)) & (iota((1, 1, ROW), 2) < n)
    value = jnp.where(at, local.astype(jnp.float32)[:, :, None], 0.0)
    rows = jnp.einsum(
        "tk,tj->kj", hit.reshape(-1, owners), value.reshape(-1, ROW), precision=lax.Precision.HIGHEST
    )
    held = jnp.clip(total - lo, 0, n)[:, None]
    lane = iota((owners, ROW), 1)
    rows = jnp.where(lane < held.astype(jnp.int32), rows, float(rows_own))
    rows = jnp.where(lane == COUNT, held, rows)
    return jnp.where(lane == SPILL, spill, rows)


def pack_kernel(slots, to_ref, cols_ref, ids_ref, out_ref):
    n = cols_ref.shape[0]

    def body(i, carry):
        at = pl.multiple_of(i * 16, 16)
        rows, to = cols_ref[pl.ds(at, 16), :], [to_ref[at + j] for j in range(16)]
        for j in range(16):
            out_ref[pl.ds(to[j], 1), :] = rows[j : j + 1, :]
        return carry

    lax.fori_loop(0, n // 16, body, 0)
    for k in range(ids_ref.shape[0]):
        at = k * slots + slots - 1
        out_ref[at : at + 1, :] = ids_ref[k : k + 1, :]


def pack(to, cols, ids, slots):
    owners = ids.shape[0]
    smem, vmem = pl.BlockSpec(memory_space=pltpu.SMEM), pl.BlockSpec(memory_space=pltpu.VMEM)
    return pl.pallas_call(
        functools.partial(pack_kernel, slots),
        out_shape=jax.ShapeDtypeStruct((owners * slots, ROW), jnp.float32),
        in_specs=[smem, vmem, vmem],
        out_specs=vmem,
        compiler_params=PARAMS,
        name="pack",
    )(to, cols, ids).reshape(owners, slots, ROW)


def add_rows(table, n, row_of, src, base):
    def body(i, carry):
        rows = src[pl.ds(pl.multiple_of(base + i * 8, 8), 8), :]
        for j in range(8):
            table[pl.ds(row_of(i * 8 + j), 1), :] += rows[j : j + 1, :]
        return carry

    lax.fori_loop(0, (n + 7) // 8, body, 0)


def strips(rows, step, body):
    def strip(i, carry):
        body(pl.multiple_of(i * step, step), step)
        return carry

    lax.fori_loop(0, rows // step, strip, 0)
    if rows % step:
        body(rows // step * step, rows % step)


def head_sum_kernel(early, id_ref, head_ref, table):
    def clear(at, n):
        table[pl.ds(at, n), :] = jnp.zeros((n, ROW), jnp.float32)

    strips(table.shape[0], 64, clear)

    def source(s, carry):
        at = s * early

        @pl.when(id_ref[at] >= 0)
        def _():
            rows = head_ref[pl.ds(pl.multiple_of(s * HEAD, HEAD), HEAD), :]
            for j in range(early):
                table[pl.ds(id_ref[at + j], 1), :] += rows[j : j + 1, :]

        return carry

    lax.fori_loop(0, head_ref.shape[0] // HEAD, source, 0)


def head_sum(head_id, head_all, rows_own, early):
    smem, vmem = pl.BlockSpec(memory_space=pltpu.SMEM), pl.BlockSpec(memory_space=pltpu.VMEM)
    return pl.pallas_call(
        functools.partial(head_sum_kernel, early),
        out_shape=jax.ShapeDtypeStruct((rows_own // 8 * 8 + 8, ROW), jnp.float32),
        in_specs=[smem, vmem],
        out_specs=vmem,
        compiler_params=PARAMS,
        cost_estimate=pl.CostEstimate(flops=10**9, bytes_accessed=6 * 10**7, transcendentals=0),
        name="head_sum",
    )(head_id, head_all)


def sum_kernel(slot_sets, *refs):
    n = len(slot_sets)
    start_ref, set_ids, set_rows = refs[0], refs[1 : 1 + n], refs[1 + n : 1 + 2 * n]
    out_ref, table, sem = refs[1 + 2 * n :]
    copy = pltpu.make_async_copy(start_ref, table, sem)
    copy.start()
    copy.wait()
    for ids_ref, rows_ref, slots in zip(set_ids, set_rows, slot_sets):

        def sender(v, carry, ids_ref=ids_ref, rows_ref=rows_ref, slots=slots):
            add_rows(table, ids_ref[v * ROW + COUNT], lambda i: ids_ref[v * ROW + i], rows_ref, v * slots)
            return carry

        lax.fori_loop(0, rows_ref.shape[0] // slots, sender, 0)

    def write(at, n):
        out_ref[pl.ds(at, n), :] = table[pl.ds(at, n), :].astype(jnp.bfloat16)

    strips(out_ref.shape[0], 64, write)


def sum_rows(start, sets, rows_own):
    smem, vmem = pl.BlockSpec(memory_space=pltpu.SMEM), pl.BlockSpec(memory_space=pltpu.VMEM)
    slot_sets = tuple(rows.shape[1] for rows in sets)
    ids = [s[:, -1, :].astype(jnp.int32).reshape(-1) for s in sets]
    rows = [s.reshape(-1, ROW) for s in sets]
    return pl.pallas_call(
        functools.partial(sum_kernel, slot_sets),
        out_shape=jax.ShapeDtypeStruct((rows_own, ROW), jnp.bfloat16),
        in_specs=[pl.BlockSpec(memory_space=pl.ANY)] + [smem] * len(sets) + [vmem] * len(sets),
        out_specs=vmem,
        scratch_shapes=[pltpu.VMEM(start.shape, jnp.float32), pltpu.SemaphoreType.DMA],
        compiler_params=PARAMS,
        name="sum_rows",
    )(start, *ids, *rows)


def local(out_grads, token_ids):
    owners, parts = lax.axis_size("vocab"), lax.axis_size("dp")
    tok = token_ids.shape[0]
    rows_own = VOCAB // owners
    cap = 3 * tok // owners
    most = cap * parts
    me = lax.axis_index("vocab")

    head_out, body_out = head(token_ids, token_ids // rows_own, out_grads, cap, owners)
    first = lax.all_to_all(head_out, "dp", split_axis=0, concat_axis=0, tiled=True)
    head_all = lax.all_gather(first.reshape(parts * HEAD, ROW), "vocab", axis=0, tiled=False)
    cols = lax.all_to_all(body_out, "dp", split_axis=0, concat_axis=0, tiled=True).reshape(-1, ROW)

    early = HEAD - 1
    ids = first[:, early, :tok].astype(jnp.int32)
    full = first[:, early, LANES + early].astype(jnp.int32)
    own, mine, hit, slot, total = plan(ids, full, early, rows_own, owners)
    row = ids - own * rows_own
    kept = SLOTS - 1
    spill = jnp.max(jnp.where(total > kept, 1.0, 0.0))
    near = id_rows(hit, slot, row, total, 0, kept, rows_own, spill)
    to = jnp.where(mine & (slot < kept), own * SLOTS + slot, kept).reshape(-1)
    arrived = lax.all_to_all(pack(to, cols, near, SLOTS), "vocab", split_axis=0, concat_axis=0, tiled=True)

    notes = head_all.reshape(owners, parts, HEAD, ROW)[:, :, early, LANES : LANES + early].astype(jnp.int32)
    head_id = notes - me * rows_own
    head_id = jnp.where((head_id >= 0) & (head_id < rows_own), head_id, -1)
    start = head_sum(head_id.reshape(-1), head_all.reshape(-1, ROW), rows_own, early)

    def short(start, arrived):
        return sum_rows(start, [arrived], rows_own)

    def long(start, arrived):
        slots = (most - kept + 8) // 8 * 8
        far = id_rows(hit, slot, row, total, kept, most, rows_own, 0.0)
        to = jnp.where(mine & (slot >= kept), own * slots + slot - kept, slots - 1).reshape(-1)
        more = lax.all_to_all(pack(to, cols, far, slots), "vocab", split_axis=0, concat_axis=0, tiled=True)
        return sum_rows(start, [arrived, more], rows_own)

    return lax.cond(jnp.max(arrived[:, -1, SPILL]) > 0, long, short, start, arrived)


def solution(mesh):
    in_specs = (P(("vocab", "dp"), None), P(("vocab", "dp")))
    out_specs = P("vocab", "dp")
    return jax.shard_map(local, mesh=mesh, in_specs=in_specs, out_specs=out_specs, check_vma=False)
```

```python
import functools

import jax
import jax.numpy as jnp
from jax import lax
from jax.experimental import pallas as pl
from jax.experimental.pallas import tpu as pltpu
from jax.sharding import PartitionSpec as P

VOCAB = 128256
LANES = 128
RING = 8
ROW = 256
HEAD = 8
SLOTS = 88
COUNT, SPILL = 254, 255
PARAMS = pltpu.CompilerParams(vmem_limit_bytes=52 * 2**20)


def iota(shape, dim):
    return lax.broadcasted_iota(jnp.int32, shape, dim)


def head_kernel(cap, ids_ref, owner_ref, ids_row_ref, x_ref, head_ref, held, sems, count_ref, pick_ref):
    tok = x_ref.shape[0]
    parts = head_ref.shape[0]
    owners, early = count_ref.shape[0], pick_ref.shape[0]
    for i in range(owners):
        count_ref[i] = 0
    for j in range(early):
        pick_ref[j] = 0

    def tally(t, full):
        o = owner_ref[t]
        c = count_ref[o] + 1
        count_ref[o] = c
        return jnp.where(c == cap, o, full)

    full = lax.fori_loop(0, tok, tally, -1)

    def pick(t, j):
        @pl.when((owner_ref[t] == full) & (j < early))
        def _():
            pick_ref[j] = t

        return j + (owner_ref[t] == full).astype(jnp.int32)

    lax.fori_loop(0, tok, pick, 0)
    copies = [
        pltpu.make_async_copy(x_ref.at[pl.ds(pick_ref[j], 1), :], held.at[j : j + 1, :], sems.at[j]) for j in range(early)
    ]
    for copy in copies:
        copy.start()
    lane = iota((1, LANES), 1)
    note = jnp.where(lane == early, full.astype(jnp.float32), 0.0)
    for j in range(early):
        note = jnp.where(lane == j, ids_ref[pick_ref[j]].astype(jnp.float32), note)
    for copy in copies:
        copy.wait()
    for d in range(parts):
        head_ref[d, 0:early, :] = held[0:early, d * ROW : (d + 1) * ROW]
        head_ref[d, early:HEAD, 0:LANES] = ids_row_ref[...]
        head_ref[d, early:HEAD, LANES:ROW] = note


def head(ids, owner, x, cap, owners):
    width = x.shape[1]
    smem, vmem = pl.BlockSpec(memory_space=pltpu.SMEM), pl.BlockSpec(memory_space=pltpu.VMEM)
    return pl.pallas_call(
        functools.partial(head_kernel, cap),
        out_shape=jax.ShapeDtypeStruct((width // ROW, HEAD, ROW), jnp.float32),
        in_specs=[smem, smem, vmem, pl.BlockSpec(memory_space=pl.ANY)],
        out_specs=vmem,
        scratch_shapes=[
            pltpu.VMEM((HEAD, width), jnp.float32),
            pltpu.SemaphoreType.DMA((HEAD - 1,)),
            pltpu.SMEM((owners,), jnp.int32),
            pltpu.SMEM((HEAD - 1,), jnp.int32),
        ],
        compiler_params=PARAMS,
        name="head",
    )(ids, owner, ids.astype(jnp.float32)[None, :], x)


def to_all(block, cols, rings, ring):
    def along_z(a, s):
        return lax.ppermute(a, "vocab", [(r * ring + i, r * ring + (i + s) % ring) for r in range(rings) for i in range(ring)])

    def along_x(a, s):
        return lax.ppermute(a, "vocab", [(r * ring + i, (r + s) % rings * ring + i) for r in range(rings) for i in range(ring)])

    near = jnp.concatenate([block] + [along_z(block, s) for s in range(1, ring)], axis=0)
    if rings != 4:
        return cols, [near] + [along_x(near, s) for s in range(1, rings)]
    cols, near = lax.optimization_barrier((cols, near))
    left, right, half = along_x(near, 1), along_x(near, -1), near.shape[0] // 2
    return cols, [near, left, right, along_x(left[:half], 1), along_x(right[half:], -1)]


def plan(ids, full, early, rows_own, owners):
    sources, tok = ids.shape
    own = ids // rows_own
    fits = own == full[:, None]
    nth = jnp.sum((fits[:, None, :] & (iota((1, tok, tok), 2) < iota((1, tok, tok), 1))).astype(jnp.int32), axis=2)
    mine = ~fits | (nth >= early)
    hit = ((own[:, :, None] == iota((1, 1, owners), 2)) & mine[:, :, None]).astype(jnp.float32)
    tri = (iota((tok, tok), 1) < iota((tok, tok), 0)).astype(jnp.float32)
    inside = jnp.einsum("ts,dsk->dtk", tri, hit)
    count = jnp.sum(hit, axis=1)
    before = jnp.sum(
        jnp.where((iota((sources, sources), 1) < iota((sources, sources), 0))[:, :, None], count[None], 0.0), axis=1
    )
    slot = jnp.sum(hit * (inside + before[:, None, :]), axis=2).astype(jnp.int32)
    total = jnp.sum(count, axis=0)
    return own, mine, hit, slot, total


def id_rows(hit, slot, local, total, lo, hi, rows_own, spill):
    n = hi - lo
    owners = hit.shape[2]
    at = (slot[:, :, None] - lo == iota((1, 1, ROW), 2)) & (iota((1, 1, ROW), 2) < n)
    value = jnp.where(at, local.astype(jnp.float32)[:, :, None], 0.0)
    rows = jnp.einsum(
        "tk,tj->kj", hit.reshape(-1, owners), value.reshape(-1, ROW), precision=lax.Precision.HIGHEST
    )
    held = jnp.clip(total - lo, 0, n)[:, None]
    lane = iota((owners, ROW), 1)
    rows = jnp.where(lane < held.astype(jnp.int32), rows, float(rows_own))
    rows = jnp.where(lane == COUNT, held, rows)
    return jnp.where(lane == SPILL, spill, rows)


def pack_kernel(slots, to_ref, cols_ref, ids_ref, out_ref):
    n = cols_ref.shape[0]

    def body(i, carry):
        at = pl.multiple_of(i * 16, 16)
        rows, to = cols_ref[pl.ds(at, 16), :], [to_ref[at + j] for j in range(16)]
        for j in range(16):
            out_ref[pl.ds(to[j], 1), :] = rows[j : j + 1, :]
        return carry

    lax.fori_loop(0, n // 16, body, 0)
    for k in range(ids_ref.shape[0]):
        at = k * slots + slots - 1
        out_ref[at : at + 1, :] = ids_ref[k : k + 1, :]


def pack(to, cols, ids, slots):
    owners = ids.shape[0]
    smem, vmem = pl.BlockSpec(memory_space=pltpu.SMEM), pl.BlockSpec(memory_space=pltpu.VMEM)
    return pl.pallas_call(
        functools.partial(pack_kernel, slots),
        out_shape=jax.ShapeDtypeStruct((owners * slots, ROW), jnp.float32),
        in_specs=[smem, vmem, vmem],
        out_specs=vmem,
        compiler_params=PARAMS,
        name="pack",
    )(to, cols, ids).reshape(owners, slots, ROW)


def add_rows(table, n, row_of, src, base):
    def body(i, carry):
        rows = src[pl.ds(pl.multiple_of(base + i * 8, 8), 8), :]
        for j in range(8):
            table[pl.ds(row_of(i * 8 + j), 1), :] += rows[j : j + 1, :]
        return carry

    lax.fori_loop(0, (n + 7) // 8, body, 0)


def strips(rows, step, body):
    def strip(i, carry):
        body(pl.multiple_of(i * step, step), step)
        return carry

    lax.fori_loop(0, rows // step, strip, 0)
    if rows % step:
        body(rows // step * step, rows % step)


def head_sum_kernel(early, id_ref, *refs):
    table = refs[-1]

    def clear(at, n):
        table[pl.ds(at, n), :] = jnp.zeros((n, ROW), jnp.float32)

    strips(table.shape[0], 64, clear)
    base = 0
    for head_ref in refs[:-1]:

        def source(s, carry, head_ref=head_ref, base=base):
            at = (base + s) * early

            @pl.when(id_ref[at] >= 0)
            def _():
                rows = head_ref[pl.ds(pl.multiple_of(s * HEAD, HEAD), HEAD), :]
                for j in range(early):
                    table[pl.ds(id_ref[at + j], 1), :] += rows[j : j + 1, :]

            return carry

        count = head_ref.shape[0] // HEAD
        lax.fori_loop(0, count, source, 0)
        base += count


def head_sum(head_id, heads, rows_own, early):
    smem, vmem = pl.BlockSpec(memory_space=pltpu.SMEM), pl.BlockSpec(memory_space=pltpu.VMEM)
    return pl.pallas_call(
        functools.partial(head_sum_kernel, early),
        out_shape=jax.ShapeDtypeStruct((rows_own // 8 * 8 + 8, ROW), jnp.float32),
        in_specs=[smem] + [vmem] * len(heads),
        out_specs=vmem,
        compiler_params=PARAMS,
        cost_estimate=pl.CostEstimate(flops=10**9, bytes_accessed=6 * 10**7, transcendentals=0),
        name="head_sum",
    )(head_id, *heads)


def sum_kernel(slot_sets, *refs):
    n = len(slot_sets)
    start_ref, set_ids, set_rows = refs[0], refs[1 : 1 + n], refs[1 + n : 1 + 2 * n]
    out_ref, table, sem = refs[1 + 2 * n :]
    copy = pltpu.make_async_copy(start_ref, table, sem)
    copy.start()
    copy.wait()
    for ids_ref, rows_ref, slots in zip(set_ids, set_rows, slot_sets):

        def sender(v, carry, ids_ref=ids_ref, rows_ref=rows_ref, slots=slots):
            add_rows(table, ids_ref[v * ROW + COUNT], lambda i: ids_ref[v * ROW + i], rows_ref, v * slots)
            return carry

        lax.fori_loop(0, rows_ref.shape[0] // slots, sender, 0)

    def write(at, n):
        out_ref[pl.ds(at, n), :] = table[pl.ds(at, n), :].astype(jnp.bfloat16)

    strips(out_ref.shape[0], 64, write)


def sum_rows(start, sets, rows_own):
    smem, vmem = pl.BlockSpec(memory_space=pltpu.SMEM), pl.BlockSpec(memory_space=pltpu.VMEM)
    slot_sets = tuple(rows.shape[1] for rows in sets)
    ids = [s[:, -1, :].astype(jnp.int32).reshape(-1) for s in sets]
    rows = [s.reshape(-1, ROW) for s in sets]
    return pl.pallas_call(
        functools.partial(sum_kernel, slot_sets),
        out_shape=jax.ShapeDtypeStruct((rows_own, ROW), jnp.bfloat16),
        in_specs=[pl.BlockSpec(memory_space=pl.ANY)] + [smem] * len(sets) + [vmem] * len(sets),
        out_specs=vmem,
        scratch_shapes=[pltpu.VMEM(start.shape, jnp.float32), pltpu.SemaphoreType.DMA],
        compiler_params=PARAMS,
        name="sum_rows",
    )(start, *ids, *rows)


def local(out_grads, token_ids):
    owners, parts = lax.axis_size("vocab"), lax.axis_size("dp")
    tok = token_ids.shape[0]
    rows_own = VOCAB // owners
    cap = 3 * tok // owners
    most = cap * parts
    me = lax.axis_index("vocab")

    head_out = head(token_ids, token_ids // rows_own, out_grads, cap, owners)
    first = lax.all_to_all(head_out, "dp", split_axis=0, concat_axis=0, tiled=True)
    cols = lax.all_to_all(out_grads, "dp", split_axis=1, concat_axis=0, tiled=True)
    cols, heads = to_all(first.reshape(parts * HEAD, ROW), cols, owners // RING, RING)

    early = HEAD - 1
    ids = first[:, early, :tok].astype(jnp.int32)
    full = first[:, early, LANES + early].astype(jnp.int32)
    own, mine, hit, slot, total = plan(ids, full, early, rows_own, owners)
    row = ids - own * rows_own
    kept = SLOTS - 1
    spill = jnp.max(jnp.where(total > kept, 1.0, 0.0))
    near = id_rows(hit, slot, row, total, 0, kept, rows_own, spill)
    to = jnp.where(mine & (slot < kept), own * SLOTS + slot, kept).reshape(-1)
    arrived = lax.all_to_all(pack(to, cols, near, SLOTS), "vocab", split_axis=0, concat_axis=0, tiled=True)

    notes = jnp.concatenate([h.reshape(-1, HEAD, ROW)[:, early, LANES : LANES + early] for h in heads])
    head_id = notes.astype(jnp.int32) - me * rows_own
    head_id = jnp.where((head_id >= 0) & (head_id < rows_own), head_id, -1)
    start = head_sum(head_id.reshape(-1), heads, rows_own, early)

    def short(start, arrived):
        return sum_rows(start, [arrived], rows_own)

    def long(start, arrived):
        slots = (most - kept + 8) // 8 * 8
        far = id_rows(hit, slot, row, total, kept, most, rows_own, 0.0)
        to = jnp.where(mine & (slot >= kept), own * slots + slot - kept, slots - 1).reshape(-1)
        more = lax.all_to_all(pack(to, cols, far, slots), "vocab", split_axis=0, concat_axis=0, tiled=True)
        return sum_rows(start, [arrived, more], rows_own)

    return lax.cond(jnp.max(arrived[:, -1, SPILL]) > 0, long, short, start, arrived)


def solution(mesh):
    in_specs = (P(("vocab", "dp"), None), P(("vocab", "dp")))
    out_specs = P("vocab", "dp")
    return jax.shard_map(local, mesh=mesh, in_specs=in_specs, out_specs=out_specs, check_vma=False)
```

```python
import functools

import jax
import jax.numpy as jnp
from jax import lax
from jax.experimental import pallas as pl
from jax.experimental.pallas import tpu as pltpu
from jax.sharding import PartitionSpec as P

VOCAB = 128256
LANES = 128
RING = 8
ROW = 256
HEAD = 8
SLOTS = 88
COUNT, SPILL = 254, 255
PARAMS = pltpu.CompilerParams(vmem_limit_bytes=52 * 2**20)


def iota(shape, dim):
    return lax.broadcasted_iota(jnp.int32, shape, dim)


def head_kernel(cap, ids_ref, owner_ref, ids_row_ref, x_ref, head_ref, held, sems, count_ref, pick_ref):
    tok = x_ref.shape[0]
    parts = head_ref.shape[0]
    owners, early = count_ref.shape[0], pick_ref.shape[0]
    for i in range(owners):
        count_ref[i] = 0
    for j in range(early):
        pick_ref[j] = 0

    def tally(t, full):
        o = owner_ref[t]
        c = count_ref[o] + 1
        count_ref[o] = c
        return jnp.where(c == cap, o, full)

    full = lax.fori_loop(0, tok, tally, -1)

    def pick(t, j):
        @pl.when((owner_ref[t] == full) & (j < early))
        def _():
            pick_ref[j] = t

        return j + (owner_ref[t] == full).astype(jnp.int32)

    lax.fori_loop(0, tok, pick, 0)
    copies = [
        pltpu.make_async_copy(x_ref.at[pl.ds(pick_ref[j], 1), :], held.at[j : j + 1, :], sems.at[j]) for j in range(early)
    ]
    for copy in copies:
        copy.start()
    lane = iota((1, LANES), 1)
    note = jnp.where(lane == early, full.astype(jnp.float32), 0.0)
    for j in range(early):
        note = jnp.where(lane == j, ids_ref[pick_ref[j]].astype(jnp.float32), note)
    for copy in copies:
        copy.wait()
    for d in range(parts):
        head_ref[d, 0:early, :] = held[0:early, d * ROW : (d + 1) * ROW]
        head_ref[d, early:HEAD, 0:LANES] = ids_row_ref[...]
        head_ref[d, early:HEAD, LANES:ROW] = note


def head(ids, owner, x, cap, owners):
    width = x.shape[1]
    smem, vmem = pl.BlockSpec(memory_space=pltpu.SMEM), pl.BlockSpec(memory_space=pltpu.VMEM)
    return pl.pallas_call(
        functools.partial(head_kernel, cap),
        out_shape=jax.ShapeDtypeStruct((width // ROW, HEAD, ROW), jnp.float32),
        in_specs=[smem, smem, vmem, pl.BlockSpec(memory_space=pl.ANY)],
        out_specs=vmem,
        scratch_shapes=[
            pltpu.VMEM((HEAD, width), jnp.float32),
            pltpu.SemaphoreType.DMA((HEAD - 1,)),
            pltpu.SMEM((owners,), jnp.int32),
            pltpu.SMEM((HEAD - 1,), jnp.int32),
        ],
        compiler_params=PARAMS,
        name="head",
    )(ids, owner, ids.astype(jnp.float32)[None, :], x)


def to_all(block, cols, rings, ring):
    def along_x(a, s):
        return lax.ppermute(a, "vocab", [(r * ring + i, (r + s) % rings * ring + i) for r in range(rings) for i in range(ring)])

    groups = [[r * ring + i for i in range(ring)] for r in range(rings)]
    half = block.shape[0] // 2
    halves = (block[:half], block[half:])
    near = [lax.all_gather(h, "vocab", axis_index_groups=groups, axis=0, tiled=True) for h in halves]
    if rings != 4:
        return cols, near + [along_x(n, s) for n in near for s in range(1, rings)]
    right = [along_x(n, 1) for n in near]
    left = [along_x(n, -1) for n in near]
    cols, near, right, left = lax.optimization_barrier((cols, near, right, left))
    return cols, near + right + left + [along_x(right[0], 1), along_x(left[1], -1)]


def plan(ids, full, early, rows_own, owners):
    sources, tok = ids.shape
    own = ids // rows_own
    fits = own == full[:, None]
    nth = jnp.sum((fits[:, None, :] & (iota((1, tok, tok), 2) < iota((1, tok, tok), 1))).astype(jnp.int32), axis=2)
    mine = ~fits | (nth >= early)
    hit = ((own[:, :, None] == iota((1, 1, owners), 2)) & mine[:, :, None]).astype(jnp.float32)
    tri = (iota((tok, tok), 1) < iota((tok, tok), 0)).astype(jnp.float32)
    inside = jnp.einsum("ts,dsk->dtk", tri, hit)
    count = jnp.sum(hit, axis=1)
    before = jnp.sum(
        jnp.where((iota((sources, sources), 1) < iota((sources, sources), 0))[:, :, None], count[None], 0.0), axis=1
    )
    slot = jnp.sum(hit * (inside + before[:, None, :]), axis=2).astype(jnp.int32)
    total = jnp.sum(count, axis=0)
    return own, mine, hit, slot, total


def id_rows(hit, slot, local, total, lo, hi, rows_own, spill):
    n = hi - lo
    owners = hit.shape[2]
    at = (slot[:, :, None] - lo == iota((1, 1, ROW), 2)) & (iota((1, 1, ROW), 2) < n)
    value = jnp.where(at, local.astype(jnp.float32)[:, :, None], 0.0)
    rows = jnp.einsum(
        "tk,tj->kj", hit.reshape(-1, owners), value.reshape(-1, ROW), precision=lax.Precision.HIGHEST
    )
    held = jnp.clip(total - lo, 0, n)[:, None]
    lane = iota((owners, ROW), 1)
    rows = jnp.where(lane < held.astype(jnp.int32), rows, float(rows_own))
    rows = jnp.where(lane == COUNT, held, rows)
    return jnp.where(lane == SPILL, spill, rows)


def pack_kernel(slots, to_ref, cols_ref, ids_ref, out_ref):
    n = cols_ref.shape[0]

    def body(i, carry):
        at = pl.multiple_of(i * 16, 16)
        rows, to = cols_ref[pl.ds(at, 16), :], [to_ref[at + j] for j in range(16)]
        for j in range(16):
            out_ref[pl.ds(to[j], 1), :] = rows[j : j + 1, :]
        return carry

    lax.fori_loop(0, n // 16, body, 0)
    for k in range(ids_ref.shape[0]):
        at = k * slots + slots - 1
        out_ref[at : at + 1, :] = ids_ref[k : k + 1, :]


def pack(to, cols, ids, slots):
    owners = ids.shape[0]
    smem, vmem = pl.BlockSpec(memory_space=pltpu.SMEM), pl.BlockSpec(memory_space=pltpu.VMEM)
    return pl.pallas_call(
        functools.partial(pack_kernel, slots),
        out_shape=jax.ShapeDtypeStruct((owners * slots, ROW), jnp.float32),
        in_specs=[smem, vmem, vmem],
        out_specs=vmem,
        compiler_params=PARAMS,
        name="pack",
    )(to, cols, ids).reshape(owners, slots, ROW)


def add_rows(table, n, row_of, src, base):
    def body(i, carry):
        rows = src[pl.ds(pl.multiple_of(base + i * 8, 8), 8), :]
        for j in range(8):
            table[pl.ds(row_of(i * 8 + j), 1), :] += rows[j : j + 1, :]
        return carry

    lax.fori_loop(0, (n + 7) // 8, body, 0)


def strips(rows, step, body):
    def strip(i, carry):
        body(pl.multiple_of(i * step, step), step)
        return carry

    lax.fori_loop(0, rows // step, strip, 0)
    if rows % step:
        body(rows // step * step, rows % step)


def head_sum_kernel(early, id_ref, *refs):
    table = refs[-1]

    def clear(at, n):
        table[pl.ds(at, n), :] = jnp.zeros((n, ROW), jnp.float32)

    strips(table.shape[0], 64, clear)
    base = 0
    for head_ref in refs[:-1]:

        def source(s, carry, head_ref=head_ref, base=base):
            at = (base + s) * early

            @pl.when(id_ref[at] >= 0)
            def _():
                rows = head_ref[pl.ds(pl.multiple_of(s * HEAD, HEAD), HEAD), :]
                for j in range(early):
                    table[pl.ds(id_ref[at + j], 1), :] += rows[j : j + 1, :]

            return carry

        count = head_ref.shape[0] // HEAD
        lax.fori_loop(0, count, source, 0)
        base += count


def head_sum(head_id, heads, rows_own, early):
    smem, vmem = pl.BlockSpec(memory_space=pltpu.SMEM), pl.BlockSpec(memory_space=pltpu.VMEM)
    return pl.pallas_call(
        functools.partial(head_sum_kernel, early),
        out_shape=jax.ShapeDtypeStruct((rows_own // 8 * 8 + 8, ROW), jnp.float32),
        in_specs=[smem] + [vmem] * len(heads),
        out_specs=vmem,
        compiler_params=PARAMS,
        cost_estimate=pl.CostEstimate(flops=10**9, bytes_accessed=6 * 10**7, transcendentals=0),
        name="head_sum",
    )(head_id, *heads)


def sum_kernel(slot_sets, *refs):
    n = len(slot_sets)
    start_ref, set_ids, set_rows = refs[0], refs[1 : 1 + n], refs[1 + n : 1 + 2 * n]
    out_ref, table, sem = refs[1 + 2 * n :]
    copy = pltpu.make_async_copy(start_ref, table, sem)
    copy.start()
    copy.wait()
    for ids_ref, rows_ref, slots in zip(set_ids, set_rows, slot_sets):

        def sender(v, carry, ids_ref=ids_ref, rows_ref=rows_ref, slots=slots):
            add_rows(table, ids_ref[v * ROW + COUNT], lambda i: ids_ref[v * ROW + i], rows_ref, v * slots)
            return carry

        lax.fori_loop(0, rows_ref.shape[0] // slots, sender, 0)

    def write(at, n):
        out_ref[pl.ds(at, n), :] = table[pl.ds(at, n), :].astype(jnp.bfloat16)

    strips(out_ref.shape[0], 64, write)


def sum_rows(start, sets, rows_own):
    smem, vmem = pl.BlockSpec(memory_space=pltpu.SMEM), pl.BlockSpec(memory_space=pltpu.VMEM)
    slot_sets = tuple(rows.shape[1] for rows in sets)
    ids = [s[:, -1, :].astype(jnp.int32).reshape(-1) for s in sets]
    rows = [s.reshape(-1, ROW) for s in sets]
    return pl.pallas_call(
        functools.partial(sum_kernel, slot_sets),
        out_shape=jax.ShapeDtypeStruct((rows_own, ROW), jnp.bfloat16),
        in_specs=[pl.BlockSpec(memory_space=pl.ANY)] + [smem] * len(sets) + [vmem] * len(sets),
        out_specs=vmem,
        scratch_shapes=[pltpu.VMEM(start.shape, jnp.float32), pltpu.SemaphoreType.DMA],
        compiler_params=PARAMS,
        name="sum_rows",
    )(start, *ids, *rows)


def local(out_grads, token_ids):
    owners, parts = lax.axis_size("vocab"), lax.axis_size("dp")
    tok = token_ids.shape[0]
    rows_own = VOCAB // owners
    cap = 3 * tok // owners
    most = cap * parts
    me = lax.axis_index("vocab")

    head_out = head(token_ids, token_ids // rows_own, out_grads, cap, owners)
    first = lax.all_to_all(head_out, "dp", split_axis=0, concat_axis=0, tiled=True)
    cols = lax.all_to_all(out_grads, "dp", split_axis=1, concat_axis=0, tiled=True)
    cols, heads = to_all(first.reshape(parts * HEAD, ROW), cols, owners // RING, RING)

    early = HEAD - 1
    ids = first[:, early, :tok].astype(jnp.int32)
    full = first[:, early, LANES + early].astype(jnp.int32)
    own, mine, hit, slot, total = plan(ids, full, early, rows_own, owners)
    row = ids - own * rows_own
    kept = SLOTS - 1
    spill = jnp.max(jnp.where(total > kept, 1.0, 0.0))
    near = id_rows(hit, slot, row, total, 0, kept, rows_own, spill)
    to = jnp.where(mine & (slot < kept), own * SLOTS + slot, kept).reshape(-1)
    arrived = lax.all_to_all(pack(to, cols, near, SLOTS), "vocab", split_axis=0, concat_axis=0, tiled=True)

    notes = jnp.concatenate([h.reshape(-1, HEAD, ROW)[:, early, LANES : LANES + early] for h in heads])
    head_id = notes.astype(jnp.int32) - me * rows_own
    head_id = jnp.where((head_id >= 0) & (head_id < rows_own), head_id, -1)
    start = head_sum(head_id.reshape(-1), heads, rows_own, early)

    def short(start, arrived):
        return sum_rows(start, [arrived], rows_own)

    def long(start, arrived):
        slots = (most - kept + 8) // 8 * 8
        far = id_rows(hit, slot, row, total, kept, most, rows_own, 0.0)
        to = jnp.where(mine & (slot >= kept), own * slots + slot - kept, slots - 1).reshape(-1)
        more = lax.all_to_all(pack(to, cols, far, slots), "vocab", split_axis=0, concat_axis=0, tiled=True)
        return sum_rows(start, [arrived, more], rows_own)

    return lax.cond(jnp.max(arrived[:, -1, SPILL]) > 0, long, short, start, arrived)


def solution(mesh):
    in_specs = (P(("vocab", "dp"), None), P(("vocab", "dp")))
    out_specs = P("vocab", "dp")
    return jax.shard_map(local, mesh=mesh, in_specs=in_specs, out_specs=out_specs, check_vma=False)
```

```python
import functools

import jax
import jax.numpy as jnp
from jax import lax
from jax.experimental import pallas as pl
from jax.experimental.pallas import tpu as pltpu
from jax.sharding import PartitionSpec as P

VOCAB = 128256
LANES = 128
RING = 8
ROW = 256
HEAD = 8
EARLY = HEAD - 1
NOTE = 8
SLOTS = 88
COUNT, SPILL = 254, 255
PARAMS = pltpu.CompilerParams(vmem_limit_bytes=52 * 2**20)


def iota(shape, dim):
    return lax.broadcasted_iota(jnp.int32, shape, dim)


def head_kernel(cap, place_ref, ids_ref, owner_ref, ids_row_ref, x_ref, head_ref, held, sems, count_ref, pick_ref):
    tok = x_ref.shape[0]
    parts = head_ref.shape[0]
    owners, early = count_ref.shape[0], EARLY
    for i in range(owners):
        count_ref[i] = 0
    for j in range(early):
        pick_ref[j] = 0

    def tally(t, full):
        o = owner_ref[t]
        c = count_ref[o] + 1
        count_ref[o] = c
        return jnp.where(c == cap, o, full)

    full = lax.fori_loop(0, tok, tally, -1)

    def pick(t, j):
        @pl.when((owner_ref[t] == full) & (j < early))
        def _():
            pick_ref[j] = t

        return j + (owner_ref[t] == full).astype(jnp.int32)

    lax.fori_loop(0, tok, pick, 0)
    copies = [
        pltpu.make_async_copy(x_ref.at[pl.ds(pick_ref[j], 1), :], held.at[j : j + 1, :], sems.at[j]) for j in range(early)
    ]
    for copy in copies:
        copy.start()
    lane = iota((1, LANES), 1) - place_ref[0] * NOTE
    note = jnp.where(lane == early, full.astype(jnp.float32), 0.0)
    for j in range(early):
        note = jnp.where(lane == j, ids_ref[pick_ref[j]].astype(jnp.float32), note)
    for copy in copies:
        copy.wait()
    for d in range(parts):
        head_ref[d, 0:early, :] = held[0:early, d * ROW : (d + 1) * ROW]
        head_ref[d, early:HEAD, 0:LANES] = ids_row_ref[...]
        head_ref[d, early:HEAD, LANES:ROW] = note


def head(place, ids, owner, x, cap, owners):
    width = x.shape[1]
    smem, vmem = pl.BlockSpec(memory_space=pltpu.SMEM), pl.BlockSpec(memory_space=pltpu.VMEM)
    return pl.pallas_call(
        functools.partial(head_kernel, cap),
        out_shape=jax.ShapeDtypeStruct((width // ROW, HEAD, ROW), jnp.float32),
        in_specs=[smem, smem, smem, vmem, pl.BlockSpec(memory_space=pl.ANY)],
        out_specs=vmem,
        scratch_shapes=[
            pltpu.VMEM((HEAD, width), jnp.float32),
            pltpu.SemaphoreType.DMA((EARLY,)),
            pltpu.SMEM((owners,), jnp.int32),
            pltpu.SMEM((EARLY,), jnp.int32),
        ],
        compiler_params=PARAMS,
        name="head",
    )(place, ids, owner, ids.astype(jnp.float32)[None, :], x)


def tight_kernel(first_ref, out_ref):
    sources = first_ref.shape[0]
    at = sources * EARLY
    out_ref[at:, :] = jnp.zeros((out_ref.shape[0] - at, ROW), jnp.float32)
    note = first_ref[0, EARLY:HEAD, LANES:ROW]
    for s in range(sources):
        out_ref[s * EARLY : (s + 1) * EARLY, :] = first_ref[s, 0:EARLY, :]
        if s:
            note += first_ref[s, EARLY:HEAD, LANES:ROW]
    out_ref[at : at + 1, LANES:ROW] = note


def tight(first):
    rows = (first.shape[0] * EARLY + 8) // 8 * 8
    vmem = pl.BlockSpec(memory_space=pltpu.VMEM)
    return pl.pallas_call(
        tight_kernel,
        out_shape=jax.ShapeDtypeStruct((rows, ROW), jnp.float32),
        in_specs=[vmem],
        out_specs=vmem,
        compiler_params=PARAMS,
        name="tight",
    )(first)


def notes_of(row, sources):
    return row[..., LANES : LANES + sources * NOTE].reshape(*row.shape[:-1], sources, NOTE)


def to_all(block, cols, rings, ring):
    def along_x(a, s):
        return lax.ppermute(a, "vocab", [(r * ring + i, (r + s) % rings * ring + i) for r in range(rings) for i in range(ring)])

    groups = [[r * ring + i for i in range(ring)] for r in range(rings)]
    near = lax.all_gather(block, "vocab", axis_index_groups=groups, axis=0, tiled=True)
    if rings != 4:
        return cols, [near] + [along_x(near, s) for s in range(1, rings)]
    cols, near, right, left = lax.optimization_barrier((cols, near, along_x(near, 1), along_x(near, -1)))
    half = near.shape[0] // 2
    return cols, [near, right, left, along_x(right[:half], 1), along_x(left[half:], -1)]


def plan(ids, full, early, rows_own, owners):
    sources, tok = ids.shape
    own = ids // rows_own
    fits = own == full[:, None]
    nth = jnp.sum((fits[:, None, :] & (iota((1, tok, tok), 2) < iota((1, tok, tok), 1))).astype(jnp.int32), axis=2)
    mine = ~fits | (nth >= early)
    hit = ((own[:, :, None] == iota((1, 1, owners), 2)) & mine[:, :, None]).astype(jnp.float32)
    tri = (iota((tok, tok), 1) < iota((tok, tok), 0)).astype(jnp.float32)
    inside = jnp.einsum("ts,dsk->dtk", tri, hit)
    count = jnp.sum(hit, axis=1)
    before = jnp.sum(
        jnp.where((iota((sources, sources), 1) < iota((sources, sources), 0))[:, :, None], count[None], 0.0), axis=1
    )
    slot = jnp.sum(hit * (inside + before[:, None, :]), axis=2).astype(jnp.int32)
    total = jnp.sum(count, axis=0)
    return own, mine, hit, slot, total


def id_rows(hit, slot, local, total, lo, hi, rows_own, spill):
    n = hi - lo
    owners = hit.shape[2]
    at = (slot[:, :, None] - lo == iota((1, 1, ROW), 2)) & (iota((1, 1, ROW), 2) < n)
    value = jnp.where(at, local.astype(jnp.float32)[:, :, None], 0.0)
    rows = jnp.einsum(
        "tk,tj->kj", hit.reshape(-1, owners), value.reshape(-1, ROW), precision=lax.Precision.HIGHEST
    )
    held = jnp.clip(total - lo, 0, n)[:, None]
    lane = iota((owners, ROW), 1)
    rows = jnp.where(lane < held.astype(jnp.int32), rows, float(rows_own))
    rows = jnp.where(lane == COUNT, held, rows)
    return jnp.where(lane == SPILL, spill, rows)


def pack_kernel(slots, to_ref, cols_ref, ids_ref, out_ref):
    n = cols_ref.shape[0]

    def body(i, carry):
        at = pl.multiple_of(i * 16, 16)
        rows, to = cols_ref[pl.ds(at, 16), :], [to_ref[at + j] for j in range(16)]
        for j in range(16):
            out_ref[pl.ds(to[j], 1), :] = rows[j : j + 1, :]
        return carry

    lax.fori_loop(0, n // 16, body, 0)
    for k in range(ids_ref.shape[0]):
        at = k * slots + slots - 1
        out_ref[at : at + 1, :] = ids_ref[k : k + 1, :]


def pack(to, cols, ids, slots):
    owners = ids.shape[0]
    smem, vmem = pl.BlockSpec(memory_space=pltpu.SMEM), pl.BlockSpec(memory_space=pltpu.VMEM)
    return pl.pallas_call(
        functools.partial(pack_kernel, slots),
        out_shape=jax.ShapeDtypeStruct((owners * slots, ROW), jnp.float32),
        in_specs=[smem, vmem, vmem],
        out_specs=vmem,
        compiler_params=PARAMS,
        name="pack",
    )(to, cols, ids).reshape(owners, slots, ROW)


def add_rows(table, n, row_of, src, base):
    def body(i, carry):
        rows = src[pl.ds(pl.multiple_of(base + i * 8, 8), 8), :]
        for j in range(8):
            table[pl.ds(row_of(i * 8 + j), 1), :] += rows[j : j + 1, :]
        return carry

    lax.fori_loop(0, (n + 7) // 8, body, 0)


def strips(rows, step, body):
    def strip(i, carry):
        body(pl.multiple_of(i * step, step), step)
        return carry

    lax.fori_loop(0, rows // step, strip, 0)
    if rows % step:
        body(rows // step * step, rows % step)


def head_sum_kernel(sources, id_ref, *refs):
    table = refs[-1]
    rows = (sources * EARLY + 8) // 8 * 8

    def clear(at, n):
        table[pl.ds(at, n), :] = jnp.zeros((n, ROW), jnp.float32)

    strips(table.shape[0], 64, clear)
    base = 0
    for head_ref in refs[:-1]:

        def block(b, carry, head_ref=head_ref, base=base):
            def source(s, carry):
                at, src = ((base + b) * sources + s) * EARLY, b * rows + s * EARLY

                @pl.when(id_ref[at] >= 0)
                def _():
                    for j in range(EARLY):
                        table[pl.ds(id_ref[at + j], 1), :] += head_ref[pl.ds(src + j, 1), :]

                return carry

            return lax.fori_loop(0, sources, source, carry)

        count = head_ref.shape[0] // rows
        lax.fori_loop(0, count, block, 0)
        base += count


def head_sum(head_id, heads, rows_own, sources):
    smem, vmem = pl.BlockSpec(memory_space=pltpu.SMEM), pl.BlockSpec(memory_space=pltpu.VMEM)
    return pl.pallas_call(
        functools.partial(head_sum_kernel, sources),
        out_shape=jax.ShapeDtypeStruct((rows_own // 8 * 8 + 8, ROW), jnp.float32),
        in_specs=[smem] + [vmem] * len(heads),
        out_specs=vmem,
        compiler_params=PARAMS,
        cost_estimate=pl.CostEstimate(flops=10**9, bytes_accessed=6 * 10**7, transcendentals=0),
        name="head_sum",
    )(head_id, *heads)


def sum_kernel(slot_sets, *refs):
    n = len(slot_sets)
    start_ref, set_ids, set_rows = refs[0], refs[1 : 1 + n], refs[1 + n : 1 + 2 * n]
    out_ref, table, sem = refs[1 + 2 * n :]
    copy = pltpu.make_async_copy(start_ref, table, sem)
    copy.start()
    copy.wait()
    for ids_ref, rows_ref, slots in zip(set_ids, set_rows, slot_sets):

        def sender(v, carry, ids_ref=ids_ref, rows_ref=rows_ref, slots=slots):
            add_rows(table, ids_ref[v * ROW + COUNT], lambda i: ids_ref[v * ROW + i], rows_ref, v * slots)
            return carry

        lax.fori_loop(0, rows_ref.shape[0] // slots, sender, 0)

    def write(at, n):
        out_ref[pl.ds(at, n), :] = table[pl.ds(at, n), :].astype(jnp.bfloat16)

    strips(out_ref.shape[0], 64, write)


def sum_rows(start, sets, rows_own):
    smem, vmem = pl.BlockSpec(memory_space=pltpu.SMEM), pl.BlockSpec(memory_space=pltpu.VMEM)
    slot_sets = tuple(rows.shape[1] for rows in sets)
    ids = [s[:, -1, :].astype(jnp.int32).reshape(-1) for s in sets]
    rows = [s.reshape(-1, ROW) for s in sets]
    return pl.pallas_call(
        functools.partial(sum_kernel, slot_sets),
        out_shape=jax.ShapeDtypeStruct((rows_own, ROW), jnp.bfloat16),
        in_specs=[pl.BlockSpec(memory_space=pl.ANY)] + [smem] * len(sets) + [vmem] * len(sets),
        out_specs=vmem,
        scratch_shapes=[pltpu.VMEM(start.shape, jnp.float32), pltpu.SemaphoreType.DMA],
        compiler_params=PARAMS,
        name="sum_rows",
    )(start, *ids, *rows)


def local(out_grads, token_ids):
    owners, parts = lax.axis_size("vocab"), lax.axis_size("dp")
    tok = token_ids.shape[0]
    rows_own = VOCAB // owners
    cap = 3 * tok // owners
    most = cap * parts
    me = lax.axis_index("vocab")

    place = lax.axis_index("dp").reshape(1)
    head_out = head(place, token_ids, token_ids // rows_own, out_grads, cap, owners)
    first = lax.all_to_all(head_out, "dp", split_axis=0, concat_axis=0, tiled=True)
    cols = lax.all_to_all(out_grads, "dp", split_axis=1, concat_axis=0, tiled=True)
    cols, heads = to_all(tight(first), cols, owners // RING, RING)

    ids = first[:, EARLY, :tok].astype(jnp.int32)
    full = notes_of(jnp.sum(first[:, EARLY, :], axis=0), parts)[:, EARLY].astype(jnp.int32)
    own, mine, hit, slot, total = plan(ids, full, EARLY, rows_own, owners)
    row = ids - own * rows_own
    kept = SLOTS - 1
    spill = jnp.max(jnp.where(total > kept, 1.0, 0.0))
    near = id_rows(hit, slot, row, total, 0, kept, rows_own, spill)
    to = jnp.where(mine & (slot < kept), own * SLOTS + slot, kept).reshape(-1)
    arrived = lax.all_to_all(pack(to, cols, near, SLOTS), "vocab", split_axis=0, concat_axis=0, tiled=True)

    rows = (parts * EARLY + 8) // 8 * 8
    notes = jnp.concatenate([notes_of(h.reshape(-1, rows, ROW)[:, parts * EARLY, :], parts)[..., :EARLY] for h in heads])
    head_id = notes.astype(jnp.int32) - me * rows_own
    head_id = jnp.where((head_id >= 0) & (head_id < rows_own), head_id, -1)
    start = head_sum(head_id.reshape(-1), heads, rows_own, parts)

    def short(start, arrived):
        return sum_rows(start, [arrived], rows_own)

    def long(start, arrived):
        slots = (most - kept + 8) // 8 * 8
        far = id_rows(hit, slot, row, total, kept, most, rows_own, 0.0)
        to = jnp.where(mine & (slot >= kept), own * slots + slot - kept, slots - 1).reshape(-1)
        more = lax.all_to_all(pack(to, cols, far, slots), "vocab", split_axis=0, concat_axis=0, tiled=True)
        return sum_rows(start, [arrived, more], rows_own)

    return lax.cond(jnp.max(arrived[:, -1, SPILL]) > 0, long, short, start, arrived)


def solution(mesh):
    in_specs = (P(("vocab", "dp"), None), P(("vocab", "dp")))
    out_specs = P("vocab", "dp")
    return jax.shard_map(local, mesh=mesh, in_specs=in_specs, out_specs=out_specs, check_vma=False)
```

```python
import functools

import jax
import jax.numpy as jnp
from jax import lax
from jax.experimental import pallas as pl
from jax.experimental.pallas import tpu as pltpu
from jax.sharding import PartitionSpec as P

VOCAB = 128256
LANES = 128
RING = 8
ROW = 256
HEAD = 8
EARLY = HEAD - 1
NOTE = 8
SLOTS = 88
COUNT, SPILL = 254, 255
PARAMS = pltpu.CompilerParams(vmem_limit_bytes=52 * 2**20)


def iota(shape, dim):
    return lax.broadcasted_iota(jnp.int32, shape, dim)


def head_kernel(cap, place_ref, ids_ref, owner_ref, ids_row_ref, x_ref, head_ref, held, sems, count_ref, pick_ref):
    tok = x_ref.shape[0]
    parts = head_ref.shape[0]
    owners, early = count_ref.shape[0], EARLY
    for i in range(owners):
        count_ref[i] = 0
    for j in range(early):
        pick_ref[j] = 0

    def tally(t, full):
        o = owner_ref[t]
        c = count_ref[o] + 1
        count_ref[o] = c
        return jnp.where(c == cap, o, full)

    full = lax.fori_loop(0, tok, tally, -1, unroll=8)

    def pick(t, j):
        @pl.when((owner_ref[t] == full) & (j < early))
        def _():
            pick_ref[j] = t

        return j + (owner_ref[t] == full).astype(jnp.int32)

    lax.fori_loop(0, tok, pick, 0, unroll=8)
    copies = [
        pltpu.make_async_copy(x_ref.at[pl.ds(pick_ref[j], 1), :], held.at[j : j + 1, :], sems.at[j]) for j in range(early)
    ]
    for copy in copies:
        copy.start()
    lane = iota((1, LANES), 1) - place_ref[0] * NOTE
    note = jnp.where(lane == early, full.astype(jnp.float32), 0.0)
    for j in range(early):
        note = jnp.where(lane == j, ids_ref[pick_ref[j]].astype(jnp.float32), note)
    for copy in copies:
        copy.wait()
    for d in range(parts):
        head_ref[d, 0:early, :] = held[0:early, d * ROW : (d + 1) * ROW]
        head_ref[d, early:HEAD, 0:LANES] = ids_row_ref[...]
        head_ref[d, early:HEAD, LANES:ROW] = note


def head(place, ids, owner, x, cap, owners):
    width = x.shape[1]
    smem, vmem = pl.BlockSpec(memory_space=pltpu.SMEM), pl.BlockSpec(memory_space=pltpu.VMEM)
    return pl.pallas_call(
        functools.partial(head_kernel, cap),
        out_shape=jax.ShapeDtypeStruct((width // ROW, HEAD, ROW), jnp.float32),
        in_specs=[smem, smem, smem, vmem, pl.BlockSpec(memory_space=pl.ANY)],
        out_specs=vmem,
        scratch_shapes=[
            pltpu.VMEM((HEAD, width), jnp.float32),
            pltpu.SemaphoreType.DMA((EARLY,)),
            pltpu.SMEM((owners,), jnp.int32),
            pltpu.SMEM((EARLY,), jnp.int32),
        ],
        compiler_params=PARAMS,
        name="head",
    )(place, ids, owner, ids.astype(jnp.float32)[None, :], x)


def tight_kernel(first_ref, out_ref):
    sources = first_ref.shape[0]
    at = sources * EARLY
    out_ref[at:, :] = jnp.zeros((out_ref.shape[0] - at, ROW), jnp.float32)
    note = first_ref[0, EARLY:HEAD, LANES:ROW]
    for s in range(sources):
        out_ref[s * EARLY : (s + 1) * EARLY, :] = first_ref[s, 0:EARLY, :]
        if s:
            note += first_ref[s, EARLY:HEAD, LANES:ROW]
    out_ref[at : at + 1, LANES:ROW] = note


def tight(first):
    rows = (first.shape[0] * EARLY + 8) // 8 * 8
    vmem = pl.BlockSpec(memory_space=pltpu.VMEM)
    return pl.pallas_call(
        tight_kernel,
        out_shape=jax.ShapeDtypeStruct((rows, ROW), jnp.float32),
        in_specs=[vmem],
        out_specs=vmem,
        compiler_params=PARAMS,
        name="tight",
    )(first)


def notes_of(row, sources):
    return row[..., LANES : LANES + sources * NOTE].reshape(*row.shape[:-1], sources, NOTE)


def along_x(a, s):
    rings = lax.axis_size("vocab") // RING
    perm = [(r * RING + i, (r + s) % rings * RING + i) for r in range(rings) for i in range(RING)]
    return lax.ppermute(a, "vocab", perm)


def along_z(block):
    rings = lax.axis_size("vocab") // RING
    groups = [[r * RING + i for i in range(RING)] for r in range(rings)]
    return lax.all_gather(block, "vocab", axis_index_groups=groups, axis=0, tiled=True)


def plan(ids, full, early, rows_own, owners):
    sources, tok = ids.shape
    own = ids // rows_own
    fits = own == full[:, None]
    nth = jnp.sum((fits[:, None, :] & (iota((1, tok, tok), 2) < iota((1, tok, tok), 1))).astype(jnp.int32), axis=2)
    mine = ~fits | (nth >= early)
    hit = ((own[:, :, None] == iota((1, 1, owners), 2)) & mine[:, :, None]).astype(jnp.float32)
    tri = (iota((tok, tok), 1) < iota((tok, tok), 0)).astype(jnp.float32)
    inside = jnp.einsum("ts,dsk->dtk", tri, hit)
    count = jnp.sum(hit, axis=1)
    before = jnp.sum(
        jnp.where((iota((sources, sources), 1) < iota((sources, sources), 0))[:, :, None], count[None], 0.0), axis=1
    )
    slot = jnp.sum(hit * (inside + before[:, None, :]), axis=2).astype(jnp.int32)
    total = jnp.sum(count, axis=0)
    return own, mine, hit, slot, total


def id_rows(hit, slot, local, total, lo, hi, rows_own, spill):
    n = hi - lo
    owners = hit.shape[2]
    at = (slot[:, :, None] - lo == iota((1, 1, ROW), 2)) & (iota((1, 1, ROW), 2) < n)
    value = jnp.where(at, local.astype(jnp.float32)[:, :, None], 0.0)
    rows = jnp.einsum(
        "tk,tj->kj", hit.reshape(-1, owners), value.reshape(-1, ROW), precision=lax.Precision.HIGHEST
    )
    held = jnp.clip(total - lo, 0, n)[:, None]
    lane = iota((owners, ROW), 1)
    rows = jnp.where(lane < held.astype(jnp.int32), rows, float(rows_own))
    rows = jnp.where(lane == COUNT, held, rows)
    return jnp.where(lane == SPILL, spill, rows)


def pack_kernel(slots, to_ref, cols_ref, ids_ref, out_ref):
    n = cols_ref.shape[0]

    def body(i, carry):
        at = pl.multiple_of(i * 16, 16)
        rows, to = cols_ref[pl.ds(at, 16), :], [to_ref[at + j] for j in range(16)]
        for j in range(16):
            out_ref[pl.ds(to[j], 1), :] = rows[j : j + 1, :]
        return carry

    lax.fori_loop(0, n // 16, body, 0)
    for k in range(ids_ref.shape[0]):
        at = k * slots + slots - 1
        out_ref[at : at + 1, :] = ids_ref[k : k + 1, :]


def pack(to, cols, ids, slots):
    owners = ids.shape[0]
    smem, vmem = pl.BlockSpec(memory_space=pltpu.SMEM), pl.BlockSpec(memory_space=pltpu.VMEM)
    return pl.pallas_call(
        functools.partial(pack_kernel, slots),
        out_shape=jax.ShapeDtypeStruct((owners * slots, ROW), jnp.float32),
        in_specs=[smem, vmem, vmem],
        out_specs=vmem,
        compiler_params=PARAMS,
        name="pack",
    )(to, cols, ids).reshape(owners, slots, ROW)


def add_rows(table, ids_ref, v, src, base):
    def body(i, carry):
        rows = src[pl.ds(pl.multiple_of(base + i * 8, 8), 8), :]
        for j in range(8):
            table[pl.ds(ids_ref[v, i * 8 + j].astype(jnp.int32), 1), :] += rows[j : j + 1, :]
        return carry

    lax.fori_loop(0, (ids_ref[v, COUNT].astype(jnp.int32) + 7) // 8, body, 0)


def strips(rows, step, body):
    def strip(i, carry):
        body(pl.multiple_of(i * step, step), step)
        return carry

    lax.fori_loop(0, rows // step, strip, 0)
    if rows % step:
        body(rows // step * step, rows % step)


def head_sum_kernel(sources, id_ref, *refs):
    table = refs[-1]
    rows = (sources * EARLY + 8) // 8 * 8

    def clear(at, n):
        table[pl.ds(at, n), :] = jnp.zeros((n, ROW), jnp.float32)

    strips(table.shape[0], 64, clear)
    base = 0
    for head_ref in refs[:-1]:

        def block(b, carry, head_ref=head_ref, base=base):
            def source(s, carry):
                at, src = ((base + b) * sources + s) * EARLY, b * rows + s * EARLY

                @pl.when(id_ref[at] >= 0)
                def _():
                    for j in range(EARLY):
                        table[pl.ds(id_ref[at + j], 1), :] += head_ref[pl.ds(src + j, 1), :]

                return carry

            return lax.fori_loop(0, sources, source, carry)

        count = head_ref.shape[0] // rows
        lax.fori_loop(0, count, block, 0)
        base += count


def head_sum(head_id, heads, rows_own, sources):
    smem, vmem = pl.BlockSpec(memory_space=pltpu.SMEM), pl.BlockSpec(memory_space=pltpu.VMEM)
    return pl.pallas_call(
        functools.partial(head_sum_kernel, sources),
        out_shape=jax.ShapeDtypeStruct((-(-(rows_own + 1) // 144) * 144, ROW), jnp.float32),
        in_specs=[smem] + [vmem] * len(heads),
        out_specs=vmem,
        compiler_params=PARAMS,
        cost_estimate=pl.CostEstimate(flops=10**9, bytes_accessed=6 * 10**7, transcendentals=0),
        name="head_sum",
    )(head_id, *heads)


def sum_kernel(n, start_ref, *refs):
    sets, out_ref, table = refs[:n], refs[n], refs[n + 1]
    held, ids, sems = refs[n + 2 : 2 * n + 2], refs[2 * n + 2 : 3 * n + 2], refs[3 * n + 2]

    @pl.when(pl.program_id(0) == 0)
    def _():
        copies = [pltpu.make_async_copy(start_ref, table, sems.at[0])]
        for k in range(n):
            last = sets[k].shape[1] - 1
            copies.append(pltpu.make_async_copy(sets[k].at[:, last, :], ids[k], sems.at[2 * k + 1]))
            copies.append(pltpu.make_async_copy(sets[k], held[k], sems.at[2 * k + 2]))
        for copy in copies:
            copy.start()
        for copy in copies:
            copy.wait()
        for k in range(n):
            senders, slots = sets[k].shape[:2]
            flat = held[k].reshape(senders * slots, ROW)

            def sender(v, carry, k=k, slots=slots, flat=flat):
                add_rows(table, ids[k], v, flat, v * slots)
                return carry

            lax.fori_loop(0, senders, sender, 0)

    base = pl.program_id(0) * out_ref.shape[0]

    def write(at, n):
        out_ref[pl.ds(at, n), :] = table[pl.ds(pl.multiple_of(base + at, 16), n), :].astype(jnp.bfloat16)

    strips(out_ref.shape[0], 48, write)


def sum_rows(start, sets, rows_own):
    hbm = pl.BlockSpec(memory_space=pl.ANY)
    block = -(-rows_own // (3 * 48)) * 48
    return pl.pallas_call(
        functools.partial(sum_kernel, len(sets)),
        grid=(3,),
        out_shape=jax.ShapeDtypeStruct((rows_own, ROW), jnp.bfloat16),
        in_specs=[hbm] * (1 + len(sets)),
        out_specs=pl.BlockSpec((block, ROW), lambda i: (i, 0)),
        scratch_shapes=[pltpu.VMEM((3 * block, ROW), jnp.float32)]
        + [pltpu.VMEM(s.shape, jnp.float32) for s in sets]
        + [pltpu.SMEM((s.shape[0], ROW), jnp.float32) for s in sets]
        + [pltpu.SemaphoreType.DMA((1 + 2 * len(sets),))],
        compiler_params=PARAMS,
        name="sum_rows",
    )(start, *sets)


def local(out_grads, token_ids):
    owners, parts = lax.axis_size("vocab"), lax.axis_size("dp")
    tok = token_ids.shape[0]
    rows_own = VOCAB // owners
    cap = 3 * tok // owners
    most = cap * parts
    me = lax.axis_index("vocab")

    place = lax.axis_index("dp").reshape(1)
    head_out = head(place, token_ids, token_ids // rows_own, out_grads, cap, owners)
    first = lax.all_to_all(head_out, "dp", split_axis=0, concat_axis=0, tiled=True)
    cols = lax.all_to_all(out_grads, "dp", split_axis=1, concat_axis=0, tiled=True)
    near = along_z(tight(first))
    right, left = along_x(near, 1), along_x(near, -1)

    ids = first[:, EARLY, :tok].astype(jnp.int32)
    full = notes_of(jnp.sum(first[:, EARLY, :], axis=0), parts)[:, EARLY].astype(jnp.int32)
    own, mine, hit, slot, total = plan(ids, full, EARLY, rows_own, owners)
    row = ids - own * rows_own
    kept = SLOTS - 1
    spill = jnp.max(jnp.where(total > kept, 1.0, 0.0))
    near_ids = id_rows(hit, slot, row, total, 0, kept, rows_own, spill)
    to = jnp.where(mine & (slot < kept), own * SLOTS + slot, kept).reshape(-1)
    packed = pack(to, cols, near_ids, SLOTS)
    packed, near, right, left = lax.optimization_barrier((packed, near, right, left))
    arrived = lax.all_to_all(packed, "vocab", split_axis=0, concat_axis=0, tiled=True)

    half = near.shape[0] // 2
    heads = [near, right, left, along_x(right[:half], 1), along_x(left[half:], -1)]
    rows = (parts * EARLY + 8) // 8 * 8
    notes = jnp.concatenate([notes_of(h.reshape(-1, rows, ROW)[:, parts * EARLY, :], parts)[..., :EARLY] for h in heads])
    head_id = notes.astype(jnp.int32) - me * rows_own
    head_id = jnp.where((head_id >= 0) & (head_id < rows_own), head_id, -1)
    start = head_sum(head_id.reshape(-1), heads, rows_own, parts)

    def short(start, arrived):
        return sum_rows(start, [arrived], rows_own)

    def long(start, arrived):
        slots = (most - kept + 8) // 8 * 8
        far = id_rows(hit, slot, row, total, kept, most, rows_own, 0.0)
        to = jnp.where(mine & (slot >= kept), own * slots + slot - kept, slots - 1).reshape(-1)
        more = lax.all_to_all(pack(to, cols, far, slots), "vocab", split_axis=0, concat_axis=0, tiled=True)
        return sum_rows(start, [arrived, more], rows_own)

    return lax.cond(jnp.max(arrived[:, -1, SPILL]) > 0, long, short, start, arrived)


def solution(mesh):
    in_specs = (P(("vocab", "dp"), None), P(("vocab", "dp")))
    out_specs = P("vocab", "dp")
    return jax.shard_map(local, mesh=mesh, in_specs=in_specs, out_specs=out_specs, check_vma=False)
```

```python
import functools

import jax
import jax.numpy as jnp
from jax import lax
from jax.experimental import pallas as pl
from jax.experimental.pallas import tpu as pltpu
from jax.sharding import PartitionSpec as P

VOCAB = 128256
LANES = 128
RING = 8
ROW = 256
HEAD = 8
EARLY = HEAD - 1
NOTE = 8
SLOTS = 88
COUNT, SPILL = 254, 255
PARAMS = pltpu.CompilerParams(vmem_limit_bytes=52 * 2**20)


def iota(shape, dim):
    return lax.broadcasted_iota(jnp.int32, shape, dim)


def head_kernel(cap, place_ref, ids_ref, owner_ref, ids_row_ref, x_ref, head_ref, held, sems, count_ref, pick_ref):
    tok = x_ref.shape[0]
    parts = head_ref.shape[0]
    owners, early = count_ref.shape[0], EARLY
    for i in range(owners):
        count_ref[i] = 0
    for j in range(early):
        pick_ref[j] = 0

    def tally(t, full):
        o = owner_ref[t]
        c = count_ref[o] + 1
        count_ref[o] = c
        return jnp.where(c == cap, o, full)

    full = lax.fori_loop(0, tok, tally, -1, unroll=8)

    def pick(t, j):
        @pl.when((owner_ref[t] == full) & (j < early))
        def _():
            pick_ref[j] = t

        return j + (owner_ref[t] == full).astype(jnp.int32)

    lax.fori_loop(0, tok, pick, 0, unroll=8)
    copies = [
        pltpu.make_async_copy(x_ref.at[pl.ds(pick_ref[j], 1), :], held.at[j : j + 1, :], sems.at[j]) for j in range(early)
    ]
    for copy in copies:
        copy.start()
    lane = iota((1, LANES), 1) - place_ref[0] * NOTE
    note = jnp.where(lane == early, full.astype(jnp.float32), 0.0)
    for j in range(early):
        note = jnp.where(lane == j, ids_ref[pick_ref[j]].astype(jnp.float32), note)
    for copy in copies:
        copy.wait()
    for d in range(parts):
        head_ref[d, 0:early, :] = held[0:early, d * ROW : (d + 1) * ROW]
        head_ref[d, early:HEAD, 0:LANES] = ids_row_ref[...]
        head_ref[d, early:HEAD, LANES:ROW] = note


def head(place, ids, owner, x, cap, owners):
    width = x.shape[1]
    smem, vmem = pl.BlockSpec(memory_space=pltpu.SMEM), pl.BlockSpec(memory_space=pltpu.VMEM)
    return pl.pallas_call(
        functools.partial(head_kernel, cap),
        out_shape=jax.ShapeDtypeStruct((width // ROW, HEAD, ROW), jnp.float32),
        in_specs=[smem, smem, smem, vmem, pl.BlockSpec(memory_space=pl.ANY)],
        out_specs=vmem,
        scratch_shapes=[
            pltpu.VMEM((HEAD, width), jnp.float32),
            pltpu.SemaphoreType.DMA((EARLY,)),
            pltpu.SMEM((owners,), jnp.int32),
            pltpu.SMEM((EARLY,), jnp.int32),
        ],
        compiler_params=PARAMS,
        name="head",
    )(place, ids, owner, ids.astype(jnp.float32)[None, :], x)


def tight_kernel(first_ref, out_ref):
    sources = first_ref.shape[0]
    at = sources * EARLY
    out_ref[at:, :] = jnp.zeros((out_ref.shape[0] - at, ROW), jnp.float32)
    note = first_ref[0, EARLY:HEAD, LANES:ROW]
    for s in range(sources):
        out_ref[s * EARLY : (s + 1) * EARLY, :] = first_ref[s, 0:EARLY, :]
        if s:
            note += first_ref[s, EARLY:HEAD, LANES:ROW]
    out_ref[at : at + 1, LANES:ROW] = note


def tight(first):
    rows = (first.shape[0] * EARLY + 8) // 8 * 8
    vmem = pl.BlockSpec(memory_space=pltpu.VMEM)
    return pl.pallas_call(
        tight_kernel,
        out_shape=jax.ShapeDtypeStruct((rows, ROW), jnp.float32),
        in_specs=[vmem],
        out_specs=vmem,
        compiler_params=PARAMS,
        name="tight",
    )(first)


def notes_of(row, sources):
    return row[..., LANES : LANES + sources * NOTE].reshape(*row.shape[:-1], sources, NOTE)


def along_x(a, s):
    rings = lax.axis_size("vocab") // RING
    perm = [(r * RING + i, (r + s) % rings * RING + i) for r in range(rings) for i in range(RING)]
    return lax.ppermute(a, "vocab", perm)


def along_z(block):
    rings = lax.axis_size("vocab") // RING
    groups = [[r * RING + i for i in range(RING)] for r in range(rings)]
    return lax.all_gather(block, "vocab", axis_index_groups=groups, axis=0, tiled=True)


def plan(ids, full, early, rows_own, owners):
    sources, tok = ids.shape
    own = ids // rows_own
    fits = own == full[:, None]
    nth = jnp.sum((fits[:, None, :] & (iota((1, tok, tok), 2) < iota((1, tok, tok), 1))).astype(jnp.int32), axis=2)
    mine = ~fits | (nth >= early)
    hit = ((own[:, :, None] == iota((1, 1, owners), 2)) & mine[:, :, None]).astype(jnp.float32)
    tri = (iota((tok, tok), 1) < iota((tok, tok), 0)).astype(jnp.float32)
    inside = jnp.einsum("ts,dsk->dtk", tri, hit)
    count = jnp.sum(hit, axis=1)
    before = jnp.sum(
        jnp.where((iota((sources, sources), 1) < iota((sources, sources), 0))[:, :, None], count[None], 0.0), axis=1
    )
    slot = jnp.sum(hit * (inside + before[:, None, :]), axis=2).astype(jnp.int32)
    total = jnp.sum(count, axis=0)
    return own, mine, hit, slot, total


def id_rows(hit, slot, local, total, lo, hi, rows_own, spill):
    n = hi - lo
    owners = hit.shape[2]
    at = (slot[:, :, None] - lo == iota((1, 1, ROW), 2)) & (iota((1, 1, ROW), 2) < n)
    value = jnp.where(at, local.astype(jnp.float32)[:, :, None], 0.0)
    rows = jnp.einsum(
        "tk,tj->kj", hit.reshape(-1, owners), value.reshape(-1, ROW), precision=lax.Precision.HIGHEST
    )
    held = jnp.clip(total - lo, 0, n)[:, None]
    lane = iota((owners, ROW), 1)
    rows = jnp.where(lane < held.astype(jnp.int32), rows, float(rows_own))
    rows = jnp.where(lane == COUNT, held, rows)
    return jnp.where(lane == SPILL, spill, rows)


def pack_kernel(slots, to_ref, cols_ref, ids_ref, out_ref):
    n = cols_ref.shape[0]

    def body(i, carry):
        at = pl.multiple_of(i * 16, 16)
        rows, to = cols_ref[pl.ds(at, 16), :], [to_ref[at + j] for j in range(16)]
        for j in range(16):
            out_ref[pl.ds(to[j], 1), :] = rows[j : j + 1, :]
        return carry

    lax.fori_loop(0, n // 16, body, 0)
    for k in range(ids_ref.shape[0]):
        at = k * slots + slots - 1
        out_ref[at : at + 1, :] = ids_ref[k : k + 1, :]


def pack(to, cols, ids, slots):
    owners = ids.shape[0]
    smem, vmem = pl.BlockSpec(memory_space=pltpu.SMEM), pl.BlockSpec(memory_space=pltpu.VMEM)
    return pl.pallas_call(
        functools.partial(pack_kernel, slots),
        out_shape=jax.ShapeDtypeStruct((owners * slots, ROW), jnp.float32),
        in_specs=[smem, vmem, vmem],
        out_specs=vmem,
        compiler_params=PARAMS,
        name="pack",
    )(to, cols, ids).reshape(owners, slots, ROW)


def add_rows(table, n, row_of, src, base):
    def body(i, carry):
        rows = src[pl.ds(pl.multiple_of(base + i * 8, 8), 8), :]
        for j in range(8):
            table[pl.ds(row_of(i * 8 + j), 1), :] += rows[j : j + 1, :]
        return carry

    lax.fori_loop(0, (n + 7) // 8, body, 0)


def strips(rows, step, body):
    def strip(i, carry):
        body(pl.multiple_of(i * step, step), step)
        return carry

    lax.fori_loop(0, rows // step, strip, 0)
    if rows % step:
        body(rows // step * step, rows % step)


def head_sum_kernel(sources, id_ref, *refs):
    table = refs[-1]
    rows = (sources * EARLY + 8) // 8 * 8

    def clear(at, n):
        table[pl.ds(at, n), :] = jnp.zeros((n, ROW), jnp.float32)

    strips(table.shape[0], 64, clear)
    base = 0
    for head_ref in refs[:-1]:

        def block(b, carry, head_ref=head_ref, base=base):
            def source(s, carry):
                at, src = ((base + b) * sources + s) * EARLY, b * rows + s * EARLY

                @pl.when(id_ref[at] >= 0)
                def _():
                    for j in range(EARLY):
                        table[pl.ds(id_ref[at + j], 1), :] += head_ref[pl.ds(src + j, 1), :]

                return carry

            return lax.fori_loop(0, sources, source, carry)

        count = head_ref.shape[0] // rows
        lax.fori_loop(0, count, block, 0)
        base += count


def head_sum(head_id, heads, rows_own, sources):
    smem, vmem = pl.BlockSpec(memory_space=pltpu.SMEM), pl.BlockSpec(memory_space=pltpu.VMEM)
    return pl.pallas_call(
        functools.partial(head_sum_kernel, sources),
        out_shape=pltpu.VMEM((rows_own // 8 * 8 + 8, ROW), jnp.float32),
        in_specs=[smem] + [vmem] * len(heads),
        out_specs=vmem,
        compiler_params=PARAMS,
        cost_estimate=pl.CostEstimate(flops=10**9, bytes_accessed=6 * 10**7, transcendentals=0),
        name="head_sum",
    )(head_id, *heads)


def sum_kernel(slot_sets, *refs):
    n = len(slot_sets)
    start_ref, set_ids, set_rows = refs[0], refs[1 : 1 + n], refs[1 + n : 1 + 2 * n]
    out_ref, table, sem = refs[1 + 2 * n :]
    copy = pltpu.make_async_copy(start_ref, table, sem)
    copy.start()
    copy.wait()
    for ids_ref, rows_ref, slots in zip(set_ids, set_rows, slot_sets):

        def sender(v, carry, ids_ref=ids_ref, rows_ref=rows_ref, slots=slots):
            add_rows(table, ids_ref[v * ROW + COUNT], lambda i: ids_ref[v * ROW + i], rows_ref, v * slots)
            return carry

        lax.fori_loop(0, rows_ref.shape[0] // slots, sender, 0)

    def write(at, n):
        out_ref[pl.ds(at, n), :] = table[pl.ds(at, n), :].astype(jnp.bfloat16)

    strips(out_ref.shape[0], 64, write)


def sum_rows(start, sets, rows_own):
    smem, vmem = pl.BlockSpec(memory_space=pltpu.SMEM), pl.BlockSpec(memory_space=pltpu.VMEM)
    slot_sets = tuple(rows.shape[1] for rows in sets)
    ids = [s[:, -1, :].astype(jnp.int32).reshape(-1) for s in sets]
    rows = [s.reshape(-1, ROW) for s in sets]
    return pl.pallas_call(
        functools.partial(sum_kernel, slot_sets),
        out_shape=pltpu.HBM((rows_own, ROW), jnp.bfloat16),
        in_specs=[pl.BlockSpec(memory_space=pl.ANY)] + [smem] * len(sets) + [vmem] * len(sets),
        out_specs=vmem,
        scratch_shapes=[pltpu.VMEM(start.shape, jnp.float32), pltpu.SemaphoreType.DMA],
        compiler_params=PARAMS,
        name="sum_rows",
    )(start, *ids, *rows)


def local(out_grads, token_ids):
    owners, parts = lax.axis_size("vocab"), lax.axis_size("dp")
    tok = token_ids.shape[0]
    rows_own = VOCAB // owners
    cap = 3 * tok // owners
    most = cap * parts
    me = lax.axis_index("vocab")

    place = lax.axis_index("dp").reshape(1)
    head_out = head(place, token_ids, token_ids // rows_own, out_grads, cap, owners)
    first = lax.all_to_all(head_out, "dp", split_axis=0, concat_axis=0, tiled=True)
    cols = lax.all_to_all(out_grads, "dp", split_axis=1, concat_axis=0, tiled=True)
    near = along_z(tight(first))
    right, left = along_x(near, 1), along_x(near, -1)

    ids = first[:, EARLY, :tok].astype(jnp.int32)
    full = notes_of(jnp.sum(first[:, EARLY, :], axis=0), parts)[:, EARLY].astype(jnp.int32)
    own, mine, hit, slot, total = plan(ids, full, EARLY, rows_own, owners)
    row = ids - own * rows_own
    kept = SLOTS - 1
    spill = jnp.max(jnp.where(total > kept, 1.0, 0.0))
    near_ids = id_rows(hit, slot, row, total, 0, kept, rows_own, spill)
    to = jnp.where(mine & (slot < kept), own * SLOTS + slot, kept).reshape(-1)
    packed = pack(to, cols, near_ids, SLOTS)
    packed, near, right, left = lax.optimization_barrier((packed, near, right, left))
    arrived = lax.all_to_all(packed, "vocab", split_axis=0, concat_axis=0, tiled=True)

    half = near.shape[0] // 2
    heads = [near, right, left, along_x(right[:half], 1), along_x(left[half:], -1)]
    rows = (parts * EARLY + 8) // 8 * 8
    notes = jnp.concatenate([notes_of(h.reshape(-1, rows, ROW)[:, parts * EARLY, :], parts)[..., :EARLY] for h in heads])
    head_id = notes.astype(jnp.int32) - me * rows_own
    head_id = jnp.where((head_id >= 0) & (head_id < rows_own), head_id, -1)
    start = head_sum(head_id.reshape(-1), heads, rows_own, parts)

    def short(start, arrived):
        return sum_rows(start, [arrived], rows_own)

    def long(start, arrived):
        slots = (most - kept + 8) // 8 * 8
        far = id_rows(hit, slot, row, total, kept, most, rows_own, 0.0)
        to = jnp.where(mine & (slot >= kept), own * slots + slot - kept, slots - 1).reshape(-1)
        more = lax.all_to_all(pack(to, cols, far, slots), "vocab", split_axis=0, concat_axis=0, tiled=True)
        return sum_rows(start, [arrived, more], rows_own)

    return lax.cond(jnp.max(arrived[:, -1, SPILL]) > 0, long, short, start, arrived)


def solution(mesh):
    in_specs = (P(("vocab", "dp"), None), P(("vocab", "dp")))
    out_specs = P("vocab", "dp")
    return jax.shard_map(local, mesh=mesh, in_specs=in_specs, out_specs=out_specs, check_vma=False)
```

```python
import functools

import jax
import jax.numpy as jnp
from jax import lax
from jax.experimental import pallas as pl
from jax.experimental.pallas import tpu as pltpu
from jax.sharding import PartitionSpec as P

VOCAB = 128256
LANES = 128
RING = 8
ROW = 256
HEAD = 8
EARLY = HEAD - 1
NOTE = 8
SLOTS = 88
COUNT, SPILL = 254, 255
PARAMS = pltpu.CompilerParams(vmem_limit_bytes=52 * 2**20)


def iota(shape, dim):
    return lax.broadcasted_iota(jnp.int32, shape, dim)


def head_kernel(cap, place_ref, ids_ref, owner_ref, ids_row_ref, x_ref, head_ref, held, sems, count_ref, pick_ref):
    tok = x_ref.shape[0]
    parts = head_ref.shape[0]
    owners, early = count_ref.shape[0], EARLY
    for i in range(owners):
        count_ref[i] = 0
    for j in range(early):
        pick_ref[j] = 0

    def tally(t, full):
        o = owner_ref[t]
        c = count_ref[o] + 1
        count_ref[o] = c
        return jnp.where(c == cap, o, full)

    full = lax.fori_loop(0, tok, tally, -1, unroll=8)

    def pick(t, j):
        @pl.when((owner_ref[t] == full) & (j < early))
        def _():
            pick_ref[j] = t

        return j + (owner_ref[t] == full).astype(jnp.int32)

    lax.fori_loop(0, tok, pick, 0, unroll=8)
    copies = [
        pltpu.make_async_copy(x_ref.at[pl.ds(pick_ref[j], 1), :], held.at[j : j + 1, :], sems.at[j]) for j in range(early)
    ]
    for copy in copies:
        copy.start()
    lane = iota((1, LANES), 1) - place_ref[0] * NOTE
    note = jnp.where(lane == early, full.astype(jnp.float32), 0.0)
    for j in range(early):
        note = jnp.where(lane == j, ids_ref[pick_ref[j]].astype(jnp.float32), note)
    for copy in copies:
        copy.wait()
    for d in range(parts):
        head_ref[d, 0:early, :] = held[0:early, d * ROW : (d + 1) * ROW]
        head_ref[d, early:HEAD, 0:LANES] = ids_row_ref[...]
        head_ref[d, early:HEAD, LANES:ROW] = note


def head(place, ids, owner, x, cap, owners):
    width = x.shape[1]
    smem, vmem = pl.BlockSpec(memory_space=pltpu.SMEM), pl.BlockSpec(memory_space=pltpu.VMEM)
    return pl.pallas_call(
        functools.partial(head_kernel, cap),
        out_shape=jax.ShapeDtypeStruct((width // ROW, HEAD, ROW), jnp.float32),
        in_specs=[smem, smem, smem, vmem, pl.BlockSpec(memory_space=pl.ANY)],
        out_specs=vmem,
        scratch_shapes=[
            pltpu.VMEM((HEAD, width), jnp.float32),
            pltpu.SemaphoreType.DMA((EARLY,)),
            pltpu.SMEM((owners,), jnp.int32),
            pltpu.SMEM((EARLY,), jnp.int32),
        ],
        compiler_params=PARAMS,
        name="head",
    )(place, ids, owner, ids.astype(jnp.float32)[None, :], x)


def tight_kernel(first_ref, out_ref):
    sources = first_ref.shape[0]
    at = sources * EARLY
    out_ref[at:, :] = jnp.zeros((out_ref.shape[0] - at, ROW), jnp.float32)
    note = first_ref[0, EARLY:HEAD, LANES:ROW]
    for s in range(sources):
        out_ref[s * EARLY : (s + 1) * EARLY, :] = first_ref[s, 0:EARLY, :]
        if s:
            note += first_ref[s, EARLY:HEAD, LANES:ROW]
    out_ref[at : at + 1, LANES:ROW] = note


def tight(first):
    rows = (first.shape[0] * EARLY + 8) // 8 * 8
    vmem = pl.BlockSpec(memory_space=pltpu.VMEM)
    return pl.pallas_call(
        tight_kernel,
        out_shape=jax.ShapeDtypeStruct((rows, ROW), jnp.float32),
        in_specs=[vmem],
        out_specs=vmem,
        compiler_params=PARAMS,
        name="tight",
    )(first)


def notes_of(row, sources):
    return row[..., LANES : LANES + sources * NOTE].reshape(*row.shape[:-1], sources, NOTE)


def along_x(a, s):
    rings = lax.axis_size("vocab") // RING
    perm = [(r * RING + i, (r + s) % rings * RING + i) for r in range(rings) for i in range(RING)]
    return lax.ppermute(a, "vocab", perm)


def along_z(block):
    rings = lax.axis_size("vocab") // RING
    groups = [[r * RING + i for i in range(RING)] for r in range(rings)]
    return lax.all_gather(block, "vocab", axis_index_groups=groups, axis=0, tiled=True)


def plan(ids, full, early, rows_own, owners):
    sources, tok = ids.shape
    own = ids // rows_own
    fits = own == full[:, None]
    nth = jnp.sum((fits[:, None, :] & (iota((1, tok, tok), 2) < iota((1, tok, tok), 1))).astype(jnp.int32), axis=2)
    mine = ~fits | (nth >= early)
    hit = ((own[:, :, None] == iota((1, 1, owners), 2)) & mine[:, :, None]).astype(jnp.float32)
    tri = (iota((tok, tok), 1) < iota((tok, tok), 0)).astype(jnp.float32)
    inside = jnp.einsum("ts,dsk->dtk", tri, hit)
    count = jnp.sum(hit, axis=1)
    before = jnp.sum(
        jnp.where((iota((sources, sources), 1) < iota((sources, sources), 0))[:, :, None], count[None], 0.0), axis=1
    )
    slot = jnp.sum(hit * (inside + before[:, None, :]), axis=2).astype(jnp.int32)
    total = jnp.sum(count, axis=0)
    return own, mine, hit, slot, total


def id_rows(hit, slot, local, total, lo, hi, rows_own, spill):
    n = hi - lo
    owners = hit.shape[2]
    at = (slot[:, :, None] - lo == iota((1, 1, ROW), 2)) & (iota((1, 1, ROW), 2) < n)
    value = jnp.where(at, local.astype(jnp.float32)[:, :, None], 0.0)
    rows = jnp.einsum(
        "tk,tj->kj", hit.reshape(-1, owners), value.reshape(-1, ROW), precision=lax.Precision.HIGHEST
    )
    held = jnp.clip(total - lo, 0, n)[:, None]
    lane = iota((owners, ROW), 1)
    rows = jnp.where(lane < held.astype(jnp.int32), rows, float(rows_own))
    rows = jnp.where(lane == COUNT, held, rows)
    return jnp.where(lane == SPILL, spill, rows)


def pack_kernel(slots, to_ref, cols_ref, ids_ref, out_ref):
    n = cols_ref.shape[0]

    def body(i, carry):
        at = pl.multiple_of(i * 16, 16)
        rows, to = cols_ref[pl.ds(at, 16), :], [to_ref[at + j] for j in range(16)]
        for j in range(16):
            out_ref[pl.ds(to[j], 1), :] = rows[j : j + 1, :]
        return carry

    lax.fori_loop(0, n // 16, body, 0)
    for k in range(ids_ref.shape[0]):
        at = k * slots + slots - 1
        out_ref[at : at + 1, :] = ids_ref[k : k + 1, :]


def pack(to, cols, ids, slots):
    owners = ids.shape[0]
    smem, vmem = pl.BlockSpec(memory_space=pltpu.SMEM), pl.BlockSpec(memory_space=pltpu.VMEM)
    return pl.pallas_call(
        functools.partial(pack_kernel, slots),
        out_shape=jax.ShapeDtypeStruct((owners * slots, ROW), jnp.float32),
        in_specs=[smem, vmem, vmem],
        out_specs=vmem,
        compiler_params=PARAMS,
        name="pack",
    )(to, cols, ids).reshape(owners, slots, ROW)


def add_rows(tables, n, row_of, src, base):
    def eight(at):
        rows, ids = src[pl.ds(pl.multiple_of(base + at, 8), 8), :], [row_of(at + j) for j in range(8)]
        for j in range(0, 8, 2):
            held = [t[pl.ds(ids[j + k], 1), :] for k, t in enumerate(tables)]
            for k, t in enumerate(tables):
                t[pl.ds(ids[j + k], 1), :] = held[k] + rows[j + k : j + k + 1, :]

    def body(i, carry):
        eight(i * 16)
        eight(i * 16 + 8)
        return carry

    eights = (n + 7) // 8
    lax.fori_loop(0, eights // 2, body, 0)

    @pl.when(eights % 2 == 1)
    def _():
        eight((eights - 1) * 8)


def strips(rows, step, body):
    def strip(i, carry):
        body(pl.multiple_of(i * step, step), step)
        return carry

    lax.fori_loop(0, rows // step, strip, 0)
    if rows % step:
        body(rows // step * step, rows % step)


def head_sum_kernel(sources, id_ref, *refs):
    table = refs[-1]
    rows = (sources * EARLY + 8) // 8 * 8

    def clear(at, n):
        table[pl.ds(at, n), :] = jnp.zeros((n, ROW), jnp.float32)

    strips(table.shape[0], 64, clear)
    base = 0
    for head_ref in refs[:-1]:

        def block(b, carry, head_ref=head_ref, base=base):
            def source(s, carry):
                at, src = ((base + b) * sources + s) * EARLY, b * rows + s * EARLY

                @pl.when(id_ref[at] >= 0)
                def _():
                    for j in range(EARLY):
                        table[pl.ds(id_ref[at + j], 1), :] += head_ref[pl.ds(src + j, 1), :]

                return carry

            return lax.fori_loop(0, sources, source, carry)

        count = head_ref.shape[0] // rows
        lax.fori_loop(0, count, block, 0)
        base += count


def head_sum(head_id, heads, rows_own, sources):
    smem, vmem = pl.BlockSpec(memory_space=pltpu.SMEM), pl.BlockSpec(memory_space=pltpu.VMEM)
    return pl.pallas_call(
        functools.partial(head_sum_kernel, sources),
        out_shape=pltpu.VMEM((rows_own // 8 * 8 + 8, ROW), jnp.float32),
        in_specs=[smem] + [vmem] * len(heads),
        out_specs=vmem,
        compiler_params=PARAMS,
        cost_estimate=pl.CostEstimate(flops=10**9, bytes_accessed=6 * 10**7, transcendentals=0),
        name="head_sum",
    )(head_id, *heads)


def sum_kernel(slot_sets, *refs):
    n = len(slot_sets)
    start_ref, set_ids, set_rows = refs[0], refs[1 : 1 + n], refs[1 + n : 1 + 2 * n]
    out_ref, table, other, sem = refs[1 + 2 * n :]
    copy = pltpu.make_async_copy(start_ref, table, sem)
    copy.start()

    def clear(at, n):
        other[pl.ds(at, n), :] = jnp.zeros((n, ROW), jnp.float32)

    strips(other.shape[0], 64, clear)
    copy.wait()
    for ids_ref, rows_ref, slots in zip(set_ids, set_rows, slot_sets):

        def sender(v, carry, ids_ref=ids_ref, rows_ref=rows_ref, slots=slots):
            add_rows((table, other), ids_ref[v * ROW + COUNT], lambda i: ids_ref[v * ROW + i], rows_ref, v * slots)
            return carry

        lax.fori_loop(0, rows_ref.shape[0] // slots, sender, 0)

    def write(at, n):
        out_ref[pl.ds(at, n), :] = (table[pl.ds(at, n), :] + other[pl.ds(at, n), :]).astype(jnp.bfloat16)

    strips(out_ref.shape[0], 64, write)


def sum_rows(start, sets, rows_own):
    smem, vmem = pl.BlockSpec(memory_space=pltpu.SMEM), pl.BlockSpec(memory_space=pltpu.VMEM)
    slot_sets = tuple(rows.shape[1] for rows in sets)
    ids = [s[:, -1, :].astype(jnp.int32).reshape(-1) for s in sets]
    rows = [s.reshape(-1, ROW) for s in sets]
    return pl.pallas_call(
        functools.partial(sum_kernel, slot_sets),
        out_shape=pltpu.HBM((rows_own, ROW), jnp.bfloat16),
        in_specs=[pl.BlockSpec(memory_space=pl.ANY)] + [smem] * len(sets) + [vmem] * len(sets),
        out_specs=vmem,
        scratch_shapes=[pltpu.VMEM(start.shape, jnp.float32)] * 2 + [pltpu.SemaphoreType.DMA],
        compiler_params=PARAMS,
        name="sum_rows",
    )(start, *ids, *rows)


def local(out_grads, token_ids):
    owners, parts = lax.axis_size("vocab"), lax.axis_size("dp")
    tok = token_ids.shape[0]
    rows_own = VOCAB // owners
    cap = 3 * tok // owners
    most = cap * parts
    me = lax.axis_index("vocab")

    place = lax.axis_index("dp").reshape(1)
    head_out = head(place, token_ids, token_ids // rows_own, out_grads, cap, owners)
    first = lax.all_to_all(head_out, "dp", split_axis=0, concat_axis=0, tiled=True)
    cols = lax.all_to_all(out_grads, "dp", split_axis=1, concat_axis=0, tiled=True)
    near = along_z(tight(first))
    right, left = along_x(near, 1), along_x(near, -1)

    ids = first[:, EARLY, :tok].astype(jnp.int32)
    full = notes_of(jnp.sum(first[:, EARLY, :], axis=0), parts)[:, EARLY].astype(jnp.int32)
    own, mine, hit, slot, total = plan(ids, full, EARLY, rows_own, owners)
    row = ids - own * rows_own
    kept = SLOTS - 1
    spill = jnp.max(jnp.where(total > kept, 1.0, 0.0))
    near_ids = id_rows(hit, slot, row, total, 0, kept, rows_own, spill)
    to = jnp.where(mine & (slot < kept), own * SLOTS + slot, kept).reshape(-1)
    packed = pack(to, cols, near_ids, SLOTS)
    packed, near, right, left = lax.optimization_barrier((packed, near, right, left))
    arrived = lax.all_to_all(packed, "vocab", split_axis=0, concat_axis=0, tiled=True)

    half = near.shape[0] // 2
    heads = [near, right, left, along_x(right[:half], 1), along_x(left[half:], -1)]
    rows = (parts * EARLY + 8) // 8 * 8
    notes = jnp.concatenate([notes_of(h.reshape(-1, rows, ROW)[:, parts * EARLY, :], parts)[..., :EARLY] for h in heads])
    head_id = notes.astype(jnp.int32) - me * rows_own
    head_id = jnp.where((head_id >= 0) & (head_id < rows_own), head_id, -1)
    start = head_sum(head_id.reshape(-1), heads, rows_own, parts)

    def short(start, arrived):
        return sum_rows(start, [arrived], rows_own)

    def long(start, arrived):
        slots = (most - kept + 8) // 8 * 8
        far = id_rows(hit, slot, row, total, kept, most, rows_own, 0.0)
        to = jnp.where(mine & (slot >= kept), own * slots + slot - kept, slots - 1).reshape(-1)
        more = lax.all_to_all(pack(to, cols, far, slots), "vocab", split_axis=0, concat_axis=0, tiled=True)
        return sum_rows(start, [arrived, more], rows_own)

    return lax.cond(jnp.max(arrived[:, -1, SPILL]) > 0, long, short, start, arrived)


def solution(mesh):
    in_specs = (P(("vocab", "dp"), None), P(("vocab", "dp")))
    out_specs = P("vocab", "dp")
    return jax.shard_map(local, mesh=mesh, in_specs=in_specs, out_specs=out_specs, check_vma=False)
```
